32 devices in a mesh: groups: 1, rows: 16 (over z, y, core), heads: 2 (over x).
Axes of the slice: x: 2, y: 2, z: 4, core: 2. Of those that a mesh axis runs over, the one named last changes fastest.
Arguments:
- queries: bfloat16 [2048, 8192], P(('groups', 'rows'), 'heads'), may hold values from -40 to 40
- passages: bfloat16 [768, 1024], P(('groups', 'rows')), may hold values from -6 to 6
- enc_gain: bfloat16 [1024], replicated, may hold values from 0.099609375 to 1.8984375
- key_weight: bfloat16 [1024, 8192], P(None, 'heads'), may hold values from -0.1875 to 0.1875
- value_weight: bfloat16 [1024, 8192], P(None, 'heads'), may hold values from -0.1875 to 0.1875
- out_weight: bfloat16 [8192, 1024], P('heads'), may hold values from -0.125 to 0.125
- passage_length: int32 [3], P('groups'), may hold values from 64 to 256, as said below
Outputs:
- cross_out: bfloat16 [2048, 1024], P(('groups', 'rows'))
The draws below stay inside these ranges and needn't reach their ends.
Inputs may be any that keep to these rules, and one draw needn't show every extreme that they name: `passage_length`: every passage has at least a quarter of its padded tokens; some passage is full and some has exactly 64 tokens.
All inputs are finite; a program needn't handle non-finite values.
Results may differ from the reference program's by a relative error of at most 0.012.
The reference program's roundings to bfloat16 on the way count: a program that leaves them out, or rounds other values in their place, can miss the bound.
Values may be sent and summed in bfloat16 or wider, within the bound.
No kernel may reach another device: no remote copies, remote signals or barrier semaphores. Data moves between devices by JAX's collectives and lax.ppermute only.
A program may use at most 128 MiB of HBM per device.

```python
import jax
import jax.numpy as jnp
from jax import lax

D = 1024
HEADS = 64
DK = 128
PASS_LEN = 256
ENC = 768
DEC = 2048
PASSAGES = 3


def draw_queries(key, part):
    first = jax.random.fold_in(key, 11)
    shape = (DEC, HEADS * DK)
    base = jnp.clip(0.25 * jax.random.normal(first, shape, jnp.float32), -1.5, 1.5)
    return base.astype(jnp.bfloat16)


def draw_passage_length(key, part):
    first = jax.random.fold_in(key, 21)
    second = jax.random.fold_in(key, 22)
    lowest_len = PASS_LEN // 4
    base = jax.random.randint(first, (PASSAGES,), lowest_len, PASS_LEN + 1)
    order = jax.random.permutation(second, PASSAGES)
    base = base.at[order[0]].set(PASS_LEN)
    base = base.at[order[1]].set(lowest_len)
    return base.astype(jnp.int32)


def steps_of(own_key, shape, pieces, low, top_value):
    factor_of, own = 1.0, jax.random.fold_in(own_key, 6)
    for position, shards_of in pieces:
        draws = jnp.exp(jax.random.uniform(jax.random.fold_in(own, position), (shards_of,), jnp.float32, low / len(pieces), top_value / len(pieces)))
        factor_of = factor_of * jnp.repeat(draws, shape[position] // shards_of).reshape([-1 if axis == position else 1 for axis in range(len(shape))])
    return factor_of


def scatter_about(key, dims, width, most, shards=(), held_as=jnp.bfloat16):
    loudness = steps_of(key, dims, shards, -0.22, 0.18) if shards else 1.0
    values = jax.random.normal(key, dims, jnp.float32) * width * loudness
    return jnp.minimum(jnp.maximum(values, -most), most).astype(held_as)


def setup_inputs(seed: int = 0, part: int = 0) -> dict:
    streams_of = jax.random.split(jax.random.key(seed), 8)
    part_splits = jax.random.split(jax.random.fold_in(streams_of[7], part), 8)
    return {
        "queries": draw_queries(jax.random.fold_in(jax.random.fold_in(streams_of[7], part), 71), part),
        "passages": scatter_about(part_splits[1], (ENC, D), 1.0, 6.0, ((0, 16),)),
        "enc_gain": jnp.clip(1.0 + 0.18 * jax.random.normal(streams_of[2], (D,), jnp.float32), 0.099609375, 1.8984375).astype(jnp.bfloat16),
        "key_weight": scatter_about(streams_of[3], (D, HEADS * DK), D ** -0.5, 0.1875, ((1, 2),)),
        "value_weight": scatter_about(streams_of[4], (D, HEADS * DK), D ** -0.5, 0.1875, ((1, 2),)),
        "out_weight": scatter_about(streams_of[5], (HEADS * DK, D), (HEADS * DK // 4) ** -0.5, 0.125, ((0, 2),)),
        "passage_length": draw_passage_length(jax.random.fold_in(jax.random.fold_in(streams_of[7], part), 71), part),
    }


LOWEST = -1e+30

def normalize(passages, enc_gain):
    wide = passages.astype(jnp.float32)
    mean_square = lax.optimization_barrier(jnp.mean(wide * wide, axis=-1, keepdims=True))
    return (wide * lax.rsqrt(mean_square + 1e-06) * enc_gain.astype(jnp.float32)).astype(jnp.bfloat16)

def reference(queries, passages, enc_gain, key_weight, value_weight, out_weight, passage_length):
    normed = normalize(passages, enc_gain)
    keys = jnp.dot(normed, key_weight, preferred_element_type=jnp.float32).astype(jnp.bfloat16)
    values = jnp.dot(normed, value_weight, preferred_element_type=jnp.float32).astype(jnp.bfloat16)
    positions = jnp.arange(ENC, dtype=jnp.int32)
    owner = positions // PASS_LEN
    valid = positions % PASS_LEN < passage_length[owner]
    key_heads = keys.reshape(ENC, HEADS, DK).transpose(1, 0, 2)
    value_heads = values.reshape(ENC, HEADS, DK).transpose(1, 0, 2)
    query_heads = queries.reshape(DEC, HEADS, DK).transpose(1, 0, 2)

    def one_head(operands):
        query_rows, key_rows, value_rows = operands
        scores = jnp.dot(query_rows, key_rows.T, preferred_element_type=jnp.float32)
        masked = jnp.where(valid[None, :], scores, LOWEST)
        top = lax.optimization_barrier(jnp.max(masked, axis=-1, keepdims=True))
        expo = jnp.where(valid[None, :], jnp.exp(scores - top), 0.0)
        denom = lax.optimization_barrier(jnp.sum(expo, axis=-1, keepdims=True))
        mixed = jnp.dot(expo.astype(jnp.bfloat16), value_rows, preferred_element_type=jnp.float32)
        return (mixed / denom).astype(jnp.bfloat16)
    attended = lax.map(one_head, (query_heads, key_heads, value_heads))
    attended = attended.transpose(1, 0, 2).reshape(DEC, HEADS * DK)
    return jnp.dot(attended, out_weight, preferred_element_type=jnp.float32).astype(jnp.bfloat16)
```

```python
import functools

import jax
import jax.numpy as jnp
from jax import lax
from jax.experimental import pallas as pl
from jax.experimental.pallas import tpu as pltpu
from jax.sharding import PartitionSpec as P

DK = 128
PASS_LEN = 256
LOWEST = -1e30
TILE = 16
HEADS_STEP = 2


def chip_cycle(chips):
    up = list(range(0, chips, 2))
    return up + [chip for chip in range(chips - 1, -1, -1) if chip % 2]


def gather_pieces(passages, number):
    chips = number // 2
    cycle = chip_cycle(chips)
    place = {chip: index for index, chip in enumerate(cycle)}

    def hop(by):
        return [
            (2 * chip + core, 2 * cycle[(place[chip] + by) % chips] + core)
            for chip in range(chips)
            for core in range(2)
        ]

    other_core = [(device, device ^ 1) for device in range(number)]
    pieces, offsets = [passages], [0]
    ahead = behind = passages
    for step in range(1, chips // 2 + 1):
        ahead = lax.ppermute(ahead, "rows", hop(1))
        pieces.append(ahead)
        offsets.append(-step)
        if 2 * step < chips:
            behind = lax.ppermute(behind, "rows", hop(-1))
            pieces.append(behind)
            offsets.append(step)
    swapped = [lax.ppermute(piece, "rows", other_core) for piece in pieces]
    owners = []
    for device in range(number):
        at, core = place[device // 2], device % 2
        from_chips = [cycle[(at + offset) % chips] for offset in offsets]
        owners.append(
            [2 * chip + core for chip in from_chips]
            + [2 * chip + 1 - core for chip in from_chips]
        )
    return pieces + swapped, owners


def kernel(cases, device_ref, length_ref, owners_ref, *refs):
    piece_refs = refs[: owners_ref.shape[1]]
    (gain_ref, own_q_ref, other_q_ref, key_ref, value_ref, out_w_ref,
     own_ref, other_ref, normed, bias, total, count, partial) = refs[owners_ref.shape[1]:]
    step = pl.program_id(0)
    rows_piece = piece_refs[0].shape[0]
    passages = length_ref.shape[0]

    @pl.when(step == 0)
    def _():
        total[...] = jnp.zeros_like(total)
        normed[...] = jnp.zeros_like(normed)
        for passage in range(passages):
            partial[passage] = -1
        device = device_ref[0]
        gain = gain_ref[...].astype(jnp.float32)
        kept = jnp.int32(0)
        for index, piece_ref in enumerate(piece_refs):
            first = owners_ref[device, index] * rows_piece
            for tile in range(rows_piece // TILE):
                row = first + tile * TILE
                passage = row // PASS_LEN
                here = length_ref[passage] - row % PASS_LEN

                @pl.when(here > 0)
                def _(kept=kept, tile=tile, piece_ref=piece_ref, here=here, passage=passage):
                    wide = piece_ref[tile * TILE:(tile + 1) * TILE, :].astype(jnp.float32)
                    mean_square = jnp.mean(wide * wide, axis=-1, keepdims=True)
                    scaled = wide * lax.rsqrt(mean_square + 1e-06) * gain
                    at = pl.multiple_of(kept * TILE, TILE)
                    normed[pl.ds(at, TILE), :] = scaled.astype(jnp.bfloat16)

                    @pl.when(here < TILE)
                    def _():
                        partial[passage] = kept * TILE + here

                kept = kept + (here > 0).astype(jnp.int32)
        count[0] = kept * TILE
        lane = lax.broadcasted_iota(jnp.int32, bias.shape, 1)
        valid = lane < kept * TILE
        for passage in range(passages):
            begin = partial[passage]
            end = (begin + TILE - 1) // TILE * TILE
            valid = valid & ((begin < 0) | (lane < begin) | (lane >= end))
        bias[...] = jnp.where(valid, 0.0, LOWEST)

    def attend(number):
        rows_in = normed[:number, :]
        key_rows = jnp.dot(
            rows_in, key_ref[...], preferred_element_type=jnp.float32
        ).astype(jnp.bfloat16)
        value_rows = jnp.dot(
            rows_in, value_ref[...], preferred_element_type=jnp.float32
        ).astype(jnp.bfloat16)
        query_rows = jnp.concatenate([own_q_ref[...], other_q_ref[...]], axis=0)
        shift = bias[0:1, :number]
        attended = []
        for head in range(HEADS_STEP):
            columns = slice(head * DK, (head + 1) * DK)
            scores = lax.dot_general(
                query_rows[:, columns], key_rows[:, columns],
                (((1,), (1,)), ((), ())), preferred_element_type=jnp.float32,
            ) + shift
            top = jnp.max(scores, axis=-1, keepdims=True)
            expo = jnp.exp(scores - top)
            denom = jnp.sum(expo, axis=-1, keepdims=True)
            mixed = jnp.dot(
                expo.astype(jnp.bfloat16), value_rows[:, columns],
                preferred_element_type=jnp.float32,
            )
            attended.append((mixed / denom).astype(jnp.bfloat16))
        total[...] += jnp.dot(
            jnp.concatenate(attended, axis=1), out_w_ref[...],
            preferred_element_type=jnp.float32,
        )

    low = 0
    for number in cases:
        pl.when((count[0] > low) & (count[0] <= number))(functools.partial(attend, number))
        low = number

    @pl.when(step == pl.num_programs(0) - 1)
    def _():
        half = own_ref.shape[0]
        own_ref[...] = total[:half, :].astype(jnp.bfloat16)
        other_ref[...] = total[half:, :].astype(jnp.bfloat16)


def on_device(number, queries, passages, enc_gain, key_weight, value_weight, out_weight, passage_length):
    rows_here, inner = queries.shape
    width = passages.shape[1]
    half = inner // 2
    steps = half // (HEADS_STEP * DK)
    block = HEADS_STEP * DK
    enc_rows = passages.shape[0] * number
    device = lax.axis_index("rows")
    core = device % 2
    other_core = [(place, place ^ 1) for place in range(number)]
    heads_axis = lax.axis_size("heads")

    given = lax.dynamic_slice_in_dim(queries, (1 - core) * half, half, axis=1)
    other_queries = lax.ppermute(given, "rows", other_core)
    pieces, owners = gather_pieces(passages, number)

    cases = [enc_rows * part // 12 // 64 * 64 for part in (6, 7, 8, 9)] + [enc_rows]
    whole = lambda shape: pl.BlockSpec(shape, lambda i, *_: (0,) * len(shape))
    own, other = pl.pallas_call(
        functools.partial(kernel, cases),
        grid_spec=pltpu.PrefetchScalarGridSpec(
            num_scalar_prefetch=3,
            grid=(steps,),
            in_specs=[whole(passages.shape)] * len(pieces) + [
                whole((1, width)),
                pl.BlockSpec((rows_here, block), lambda i, d, *_: (0, d[0] % 2 * steps + i)),
                pl.BlockSpec((rows_here, block), lambda i, *_: (0, i)),
                pl.BlockSpec((width, block), lambda i, d, *_: (0, d[0] % 2 * steps + i)),
                pl.BlockSpec((width, block), lambda i, d, *_: (0, d[0] % 2 * steps + i)),
                pl.BlockSpec((block, width), lambda i, d, *_: (d[0] % 2 * steps + i, 0)),
            ],
            out_specs=[whole((rows_here, width))] * 2,
            scratch_shapes=[
                pltpu.VMEM((enc_rows, width), jnp.bfloat16),
                pltpu.VMEM((8, enc_rows), jnp.float32),
                pltpu.VMEM((2 * rows_here, width), jnp.float32),
                pltpu.SMEM((1,), jnp.int32),
                pltpu.SMEM((passage_length.shape[0],), jnp.int32),
            ],
        ),
        out_shape=[jax.ShapeDtypeStruct((rows_here, width), jnp.bfloat16)] * 2,
        compiler_params=pltpu.CompilerParams(vmem_limit_bytes=40 * 1024 * 1024),
        name="attention",
    )(
        device.reshape(1), passage_length, jnp.array(owners, jnp.int32), *pieces,
        enc_gain.reshape(1, width), queries, other_queries, key_weight, value_weight, out_weight,
    )
    received = lax.ppermute(other, "rows", other_core)
    share = (own.astype(jnp.float32) + received.astype(jnp.float32)).astype(jnp.bfloat16)
    by = 1
    while by < heads_axis:
        turn = [(place, place ^ by) for place in range(heads_axis)]
        given = lax.ppermute(share, "heads", turn)
        share = (share.astype(jnp.float32) + given.astype(jnp.float32)).astype(jnp.bfloat16)
        by *= 2
    return share


def solution(mesh):
    return jax.shard_map(
        functools.partial(on_device, mesh.shape["rows"]),
        mesh=mesh,
        in_specs=(
            P(("groups", "rows"), "heads"),
            P(("groups", "rows"), None),
            P(),
            P(None, "heads"),
            P(None, "heads"),
            P("heads", None),
            P("groups"),
        ),
        out_specs=P(("groups", "rows"), None),
        check_vma=False,
    )
```

```python
import functools

import jax
import jax.numpy as jnp
from jax import lax
from jax.experimental import pallas as pl
from jax.experimental.pallas import tpu as pltpu
from jax.sharding import PartitionSpec as P

DK = 128
PASS_LEN = 256
LOWEST = -1e30
TILE = 16
WIDE = 1024
HEADS_STEP = 8
ON_CHIP = pl.BlockSpec(memory_space=pltpu.VMEM)
SCALARS = pl.BlockSpec(memory_space=pltpu.SMEM)
FAR = pl.BlockSpec(memory_space=pltpu.HBM)


def params(mib):
    return pltpu.CompilerParams(vmem_limit_bytes=mib * 1024 * 1024)


def cost(flops, moved, exps=0):
    return pl.CostEstimate(flops=flops, bytes_accessed=moved, transcendentals=exps)


def chip_cycle(chips):
    up = list(range(0, chips, 2))
    return up + [chip for chip in range(chips - 1, -1, -1) if chip % 2]


def owner_of(device, source, chips):
    offset, crossed = source
    chip, core = device >> 1, device & 1
    place = jnp.where((chip & 1) == 0, chip >> 1, chips - ((chip + 1) >> 1)) + offset
    place = jnp.where(place < 0, place + chips, jnp.where(place >= chips, place - chips, place))
    chip = jnp.where(place < (chips + 1) >> 1, place << 1, ((chips - place) << 1) - 1)
    return (chip << 1) + (core ^ crossed)


class Plan:
    def __init__(self, order, rows_piece, passages):
        self.order, self.per_piece = order, rows_piece // TILE
        self.rows_piece, self.passages = rows_piece, passages
        self.tiles = len(order) * self.per_piece
        self.size = 2 * self.tiles + 2 + passages

    def write(self, plan, device, length_ref, chips):
        shift = PASS_LEN.bit_length() - 1
        for passage in range(self.passages):
            plan[2 * self.tiles + 2 + passage] = -1
        kept = jnp.int32(0)
        for index, source in enumerate(self.order):
            first = owner_of(device, source, chips) * self.rows_piece
            for tile in range(index * self.per_piece, (index + 1) * self.per_piece):
                row = first + (tile - index * self.per_piece) * TILE
                passage = row >> shift
                here = length_ref[passage] - (row & (PASS_LEN - 1))
                plan[tile] = here
                plan[self.tiles + tile] = kept

                @pl.when((here > 0) & (here < TILE))
                def _(kept=kept, here=here, passage=passage):
                    plan[2 * self.tiles + 2 + passage] = kept * TILE + here

                kept = kept + (here > 0).astype(jnp.int32)
        plan[2 * self.tiles] = kept
        plan[2 * self.tiles + 1] = device & 1

    def here(self, plan, tile):
        return plan[tile]

    def place(self, plan, tile):
        return plan[self.tiles + tile]

    def total(self, plan):
        return plan[2 * self.tiles]

    def core(self, plan):
        return plan[2 * self.tiles + 1]

    def partial(self, plan, passage):
        return plan[2 * self.tiles + 2 + passage]


def keep_valid(layout, plan, first, piece_refs, raw):
    begin = layout.place(plan, first * layout.per_piece)
    after = (first + len(piece_refs)) * layout.per_piece
    for index, piece_ref in enumerate(piece_refs):
        for tile in range(layout.per_piece):
            at = (first + index) * layout.per_piece + tile

            @pl.when(layout.here(plan, at) > 0)
            def _(at=at, tile=tile, piece_ref=piece_ref):
                row = pl.multiple_of((layout.place(plan, at) - begin) * TILE, TILE)
                raw[pl.ds(row, TILE), :] = piece_ref[tile * TILE:(tile + 1) * TILE, :]

    end = layout.place(plan, after) if after < layout.tiles else layout.total(plan)
    return begin, end - begin


def normalize(raw, rows, gain_ref, kept, number):
    wide = raw[:number, :].astype(jnp.float32)
    mean_square = jnp.mean(wide * wide, axis=-1, keepdims=True)
    scaled = wide * lax.rsqrt(mean_square + 1e-06) * gain_ref[...].astype(jnp.float32).reshape(1, -1)
    row = lax.broadcasted_iota(jnp.int32, scaled.shape, 0)
    rows[:number, :] = jnp.where(row < kept * TILE, scaled, 0.0).astype(jnp.bfloat16)


def stage_kernel(axis, device_ref, far, near, sem):
    half = near.shape[axis]
    ours = pl.ds(pl.multiple_of((device_ref[0] & 1) * half, half), half)
    copy = pltpu.make_async_copy(far.at[(slice(None),) * axis + (ours,)], near, sem)
    copy.start()
    copy.wait()


def stage(device, weight, axis):
    shape = tuple(size // 2 if at == axis else size for at, size in enumerate(weight.shape))
    return pl.pallas_call(
        functools.partial(stage_kernel, axis),
        in_specs=[SCALARS, FAR],
        out_specs=ON_CHIP,
        out_shape=jax.ShapeDtypeStruct(shape, weight.dtype),
        scratch_shapes=[pltpu.SemaphoreType.DMA],
        compiler_params=params(48),
        cost_estimate=cost(0, 2 * weight.size),
        name="stage",
    )(device, weight)


def begin_kernel(layout, chips, device_ref, length_far, gain_far, key_w_ref, value_far, queries_far, own_far,
                 crossed_ref, plan, gain_ref, value_w_ref, keys_ref, values_ref, own_q_ref, given_q_ref,
                 length_ref, own_ref, raw, rows, sems):
    device = device_ref[0]
    half = value_w_ref.shape[1]
    ours = pl.ds(pl.multiple_of((device & 1) * half, half), half)
    theirs = pl.ds(pl.multiple_of((1 - (device & 1)) * half, half), half)
    moves = (
        (length_far, length_ref),
        (own_far, own_ref),
        (gain_far, gain_ref),
        (value_far.at[:, ours], value_w_ref),
        (queries_far.at[:, ours], own_q_ref),
        (queries_far.at[:, theirs], given_q_ref),
    )
    copies = [
        pltpu.make_async_copy(source, target, sems.at[index])
        for index, (source, target) in enumerate(moves)
    ]
    for copy in copies:
        copy.start()
    copies[0].wait()
    layout.write(plan, device, length_ref, chips)
    copies[1].wait()
    _, kept = keep_valid(layout, plan, 0, [own_ref, crossed_ref], raw)
    copies[2].wait()
    number = raw.shape[0]
    normalize(raw, rows, gain_ref, kept, number)
    for weight_ref, out_ref in ((key_w_ref, keys_ref), (value_w_ref, values_ref)):
        if weight_ref is value_w_ref:
            for copy in copies[3:]:
                copy.wait()
        for left in range(0, half, WIDE):
            columns = slice(left, min(left + WIDE, half))
            out_ref[:number, columns] = jnp.dot(
                rows[...], weight_ref[:, columns], preferred_element_type=jnp.float32
            ).astype(jnp.bfloat16)


def begin(layout, chips, device, passage_length, gain, key_w, value_weight, queries, own, crossed, held_rows):
    width, half = key_w.shape
    held = jax.ShapeDtypeStruct((held_rows, half), jnp.bfloat16)
    query_half = jax.ShapeDtypeStruct((queries.shape[0], half), queries.dtype)
    return pl.pallas_call(
        functools.partial(begin_kernel, layout, chips),
        in_specs=[SCALARS, FAR, FAR, ON_CHIP, FAR, FAR, FAR, ON_CHIP],
        out_specs=[SCALARS] + [ON_CHIP] * 6,
        out_shape=[
            jax.ShapeDtypeStruct((layout.size,), jnp.int32),
            jax.ShapeDtypeStruct(gain.shape, gain.dtype),
            jax.ShapeDtypeStruct(key_w.shape, key_w.dtype),
            held, held, query_half, query_half,
        ],
        scratch_shapes=[
            pltpu.SMEM(passage_length.shape, jnp.int32),
            pltpu.VMEM(own.shape, own.dtype),
            pltpu.VMEM((2 * own.shape[0], width), jnp.bfloat16),
            pltpu.VMEM((2 * own.shape[0], width), jnp.bfloat16),
            pltpu.SemaphoreType.DMA((6,)),
        ],
        compiler_params=params(36),
        cost_estimate=cost(8 * own.shape[0] * width * half, 8 * width * half),
        name="begin",
    )(device, passage_length, gain, key_w, value_weight, queries, own, crossed)


def project_kernel(layout, first, count, cases, stages, plan, gain_ref, key_w_ref, value_w_ref, *refs):
    piece_refs = refs[:count]
    if stages:
        out_far, out_w_ref, sem = refs[count], refs[-4], refs[-1]
        refs = refs[:-4] + refs[-3:-1]
        half = out_w_ref.shape[0]
        ours = pl.ds(pl.multiple_of(layout.core(plan) * half, half), half)
        staging = pltpu.make_async_copy(out_far.at[ours, :], out_w_ref, sem)
        staging.start()
    keys_ref, values_ref, raw, rows = refs[-4:]
    begin_tile, kept = keep_valid(layout, plan, first, piece_refs, raw)
    start = pl.multiple_of(begin_tile * TILE, TILE)
    width = key_w_ref.shape[1]

    def project(number):
        normalize(raw, rows, gain_ref, kept, number)
        for left in range(0, width, WIDE):
            columns = slice(left, min(left + WIDE, width))
            for weight_ref, out_ref in ((key_w_ref, keys_ref), (value_w_ref, values_ref)):
                out_ref[pl.ds(start, number), columns] = jnp.dot(
                    rows[:number, :], weight_ref[:, columns], preferred_element_type=jnp.float32
                ).astype(jnp.bfloat16)

    low = 0
    for number in cases:
        pl.when((kept * TILE > low) & (kept * TILE <= number))(functools.partial(project, number))
        low = number
    if stages:
        staging.wait()


def project(layout, first, plan, gain, key_w, value_w, pieces, held, out_weight=None):
    rows_now = len(pieces) * layout.rows_piece
    width, half = key_w.shape
    cases = sorted({-(-rows_now * part // 3 // TILE) * TILE for part in (2, 3)})
    stages = out_weight is not None
    shapes = [jax.ShapeDtypeStruct(held[0].shape, jnp.bfloat16)] * 2
    if stages:
        shapes.append(jax.ShapeDtypeStruct((half, out_weight.shape[1]), out_weight.dtype))
    at = 4 + len(pieces) + stages
    return pl.pallas_call(
        functools.partial(project_kernel, layout, first, len(pieces), cases, stages),
        in_specs=[SCALARS] + [ON_CHIP] * (3 + len(pieces)) + [FAR] * stages + [ON_CHIP] * 2,
        out_specs=[ON_CHIP] * len(shapes),
        out_shape=shapes,
        scratch_shapes=[pltpu.VMEM((rows_now, width), jnp.bfloat16)] * 2 + [pltpu.SemaphoreType.DMA] * stages,
        input_output_aliases={at: 0, at + 1: 1},
        compiler_params=params(28 if stages else 16),
        cost_estimate=cost(4 * rows_now * width * half, 4 * width * half),
        name="project",
    )(plan, gain, key_w, value_w, *pieces, *([out_weight] if stages else []), *held)


def attend_kernel(layout, cases, plan, own_q_ref, other_q_ref, keys_ref, values_ref, out_w_ref,
                  own_ref, other_ref, bias, total):
    half, inner = own_q_ref.shape
    kept = layout.total(plan)
    lane = lax.broadcasted_iota(jnp.int32, bias.shape, 1)
    valid = lane < kept * TILE
    for passage in range(layout.passages):
        begin = layout.partial(plan, passage)
        end = ((begin + TILE - 1) >> (TILE.bit_length() - 1)) * TILE
        valid = valid & ((begin < 0) | (lane < begin) | (lane >= end))
    bias[...] = jnp.where(valid, 0.0, LOWEST)

    def attend_heads(number, count, left):
        columns = pl.ds(left, count * DK)
        query_rows = jnp.concatenate([own_q_ref[:, columns], other_q_ref[:, columns]], axis=0)
        key_rows, value_rows = keys_ref[:number, columns], values_ref[:number, columns]
        attended = []
        for head in range(count):
            here = slice(head * DK, (head + 1) * DK)
            scores = lax.dot_general(
                query_rows[:, here], key_rows[:, here],
                (((1,), (1,)), ((), ())), preferred_element_type=jnp.float32,
            ) + bias[0:1, :number]
            top = jnp.max(scores, axis=-1, keepdims=True)
            expo = jnp.exp(scores - top)
            denom = jnp.sum(expo, axis=-1, keepdims=True)
            mixed = jnp.dot(
                expo.astype(jnp.bfloat16), value_rows[:, here], preferred_element_type=jnp.float32
            )
            attended.append((mixed / denom).astype(jnp.bfloat16))
        return jnp.concatenate(attended, axis=1)

    def attend(number, count):
        def clear(tile, carry):
            at = pl.ds(pl.multiple_of(tile * TILE, TILE), TILE)
            keys_ref[at, :] = jnp.zeros((TILE, inner), jnp.bfloat16)
            values_ref[at, :] = jnp.zeros((TILE, inner), jnp.bfloat16)
            return carry

        lax.fori_loop(kept, number // TILE, clear, 0)

        def heads(step, carry):
            left = pl.multiple_of(step * count * DK, count * DK)
            attended = attend_heads(number, count, left)
            product = jnp.dot(attended, out_w_ref[pl.ds(left, count * DK), :], preferred_element_type=jnp.float32)

            @pl.when(step == 0)
            def _():
                total[...] = product

            @pl.when(step > 0)
            def _():
                total[...] += product

            return carry

        lax.fori_loop(0, inner // (count * DK), heads, 0)

    low = 0
    for number in cases:
        count = 1 if number == cases[-1] else HEADS_STEP
        pl.when((kept * TILE > low) & (kept * TILE <= number))(functools.partial(attend, number, count))
        low = number
    own_ref[...] = total[:half, :].astype(jnp.bfloat16)
    other_ref[...] = total[half:, :].astype(jnp.bfloat16)


def attend(layout, plan, own_q, other_q, keys, values, out_w):
    rows_here, half = own_q.shape
    width = out_w.shape[1]
    enc_rows = layout.tiles * TILE
    cases = [enc_rows * part // 12 // 64 * 64 for part in (8, 9)] + [enc_rows]
    return pl.pallas_call(
        functools.partial(attend_kernel, layout, cases),
        in_specs=[SCALARS] + [ON_CHIP] * 5,
        out_specs=[ON_CHIP] * 2,
        out_shape=[jax.ShapeDtypeStruct((rows_here, width), jnp.bfloat16)] * 2,
        scratch_shapes=[
            pltpu.VMEM((8, enc_rows), jnp.float32),
            pltpu.VMEM((2 * rows_here, width), jnp.float32),
        ],
        compiler_params=params(24),
        cost_estimate=cost(4 * rows_here * (2 * enc_rows + width) * half, 2 * half * width),
        name="attend",
    )(plan, own_q, other_q, keys, values, out_w)


def on_device(number, queries, passages, enc_gain, key_weight, value_weight, out_weight, passage_length):
    rows_piece = passages.shape[0]
    heads_axis = lax.axis_size("heads")
    chips = number // 2
    cycle = chip_cycle(chips)
    place = {chip: index for index, chip in enumerate(cycle)}
    other_core = [(device, device ^ 1) for device in range(number)]

    def hop(by, crossed=0):
        return [
            (2 * chip + core, 2 * cycle[(place[chip] + by) % chips] + (core ^ crossed))
            for chip in range(chips)
            for core in range(2)
        ]

    def cross(piece):
        return lax.ppermute(piece, "rows", other_core)

    rounds = []
    for step in range(1, chips // 2 + 1):
        if 2 * step == chips:
            rounds.append([(-step, 0), (step, 1)])
        else:
            rounds.append([(-step, 0), (step, 0), (-step, 1), (step, 1)])
    order = [(0, 0), (0, 1)] + [source for sources in rounds for source in sources]
    layout = Plan(order, rows_piece, passage_length.shape[0])

    device = lax.axis_index("rows").reshape(1)
    held_rows = number * rows_piece + 4 * rows_piece
    key_w = stage(device, key_weight, 1)
    plan, gain, value_w, *held, own_q, given_q = begin(
        layout, chips, device, passage_length, enc_gain, key_w, value_weight,
        queries, passages, cross(passages), held_rows,
    )
    other_q = cross(given_q)

    ahead = lax.ppermute(passages, "rows", hop(1))
    behind = lax.ppermute(passages, "rows", hop(-1, len(rounds[0]) == 2))
    first, out_w = 2, None
    staged_by = max(0, len(rounds) - 2)
    for index, (sources, later) in enumerate(zip(rounds, rounds[1:] + [None])):
        ahead, behind, *held = lax.optimization_barrier((ahead, behind, *held))
        pieces = [ahead, behind]
        if len(sources) > 2:
            pieces += [cross(ahead), cross(behind)]
        if later:
            ahead = lax.ppermute(ahead, "rows", hop(1))
            behind = lax.ppermute(behind, "rows", hop(-1, len(later) == 2))
        *held, last = project(
            layout, first, plan, gain, key_w, value_w, pieces, held, out_weight if index == staged_by else None
        )
        if index == staged_by:
            out_w = last
        else:
            held.append(last)
        first += len(pieces)
    keys, values = held

    own, other = attend(layout, plan, own_q, other_q, keys, values, out_w)
    share = (own.astype(jnp.float32) + cross(other).astype(jnp.float32)).astype(jnp.bfloat16)
    by = 1
    while by < heads_axis:
        turn = [(place, place ^ by) for place in range(heads_axis)]
        given = lax.ppermute(share, "heads", turn)
        share = (share.astype(jnp.float32) + given.astype(jnp.float32)).astype(jnp.bfloat16)
        by *= 2
    return share


def solution(mesh):
    return jax.shard_map(
        functools.partial(on_device, mesh.shape["rows"]),
        mesh=mesh,
        in_specs=(
            P(("groups", "rows"), "heads"),
            P(("groups", "rows"), None),
            P(),
            P(None, "heads"),
            P(None, "heads"),
            P("heads", None),
            P("groups"),
        ),
        out_specs=P(("groups", "rows"), None),
        check_vma=False,
    )
```

```python
import functools

import jax
import jax.numpy as jnp
from jax import lax
from jax.experimental import pallas as pl
from jax.experimental.pallas import tpu as pltpu
from jax.sharding import PartitionSpec as P

DK = 128
PASS_LEN = 256
LOWEST = -1e30
TILE = 16
WIDE = 1024
ON_CHIP = pl.BlockSpec(memory_space=pltpu.VMEM)
SCALARS = pl.BlockSpec(memory_space=pltpu.SMEM)
FAR = pl.BlockSpec(memory_space=pltpu.HBM)


def params(mib):
    return pltpu.CompilerParams(vmem_limit_bytes=mib * 1024 * 1024)


def cost(flops, moved, exps=0):
    return pl.CostEstimate(flops=flops, bytes_accessed=moved, transcendentals=exps)


def chip_cycle(chips):
    up = list(range(0, chips, 2))
    return up + [chip for chip in range(chips - 1, -1, -1) if chip % 2]


def owner_of(device, source, chips):
    offset, crossed = source
    chip, core = device >> 1, device & 1
    place = jnp.where((chip & 1) == 0, chip >> 1, chips - ((chip + 1) >> 1)) + offset
    place = jnp.where(place < 0, place + chips, jnp.where(place >= chips, place - chips, place))
    chip = jnp.where(place < (chips + 1) >> 1, place << 1, ((chips - place) << 1) - 1)
    return (chip << 1) + (core ^ crossed)


class Plan:
    def __init__(self, order, rows_piece, passages):
        self.order, self.per_piece = order, rows_piece // TILE
        self.rows_piece, self.passages = rows_piece, passages
        self.tiles = len(order) * self.per_piece
        self.size = 2 * self.tiles + 2 + passages

    def write(self, plan, device, length_ref, chips):
        shift = PASS_LEN.bit_length() - 1
        for passage in range(self.passages):
            plan[2 * self.tiles + 2 + passage] = -1
        kept = jnp.int32(0)
        for index, source in enumerate(self.order):
            first = owner_of(device, source, chips) * self.rows_piece
            for tile in range(index * self.per_piece, (index + 1) * self.per_piece):
                row = first + (tile - index * self.per_piece) * TILE
                passage = row >> shift
                here = length_ref[passage] - (row & (PASS_LEN - 1))
                plan[tile] = here
                plan[self.tiles + tile] = kept

                @pl.when((here > 0) & (here < TILE))
                def _(kept=kept, here=here, passage=passage):
                    plan[2 * self.tiles + 2 + passage] = kept * TILE + here

                kept = kept + (here > 0).astype(jnp.int32)
        plan[2 * self.tiles] = kept
        plan[2 * self.tiles + 1] = device & 1

    def here(self, plan, tile):
        return plan[tile]

    def place(self, plan, tile):
        return plan[self.tiles + tile]

    def total(self, plan):
        return plan[2 * self.tiles]

    def core(self, plan):
        return plan[2 * self.tiles + 1]

    def partial(self, plan, passage):
        return plan[2 * self.tiles + 2 + passage]


def keep_valid(layout, plan, first, piece_refs, raw):
    begin = layout.place(plan, first * layout.per_piece)
    after = (first + len(piece_refs)) * layout.per_piece
    for index, piece_ref in enumerate(piece_refs):
        for tile in range(layout.per_piece):
            at = (first + index) * layout.per_piece + tile

            @pl.when(layout.here(plan, at) > 0)
            def _(at=at, tile=tile, piece_ref=piece_ref):
                row = pl.multiple_of((layout.place(plan, at) - begin) * TILE, TILE)
                raw[pl.ds(row, TILE), :] = piece_ref[tile * TILE:(tile + 1) * TILE, :]

    end = layout.place(plan, after) if after < layout.tiles else layout.total(plan)
    return begin, end - begin


def normalize(raw, rows, gain_ref, kept, number):
    wide = raw[:number, :].astype(jnp.float32)
    mean_square = jnp.mean(wide * wide, axis=-1, keepdims=True)
    scaled = wide * lax.rsqrt(mean_square + 1e-06) * gain_ref[...].astype(jnp.float32).reshape(1, -1)
    row = lax.broadcasted_iota(jnp.int32, scaled.shape, 0)
    rows[:number, :] = jnp.where(row < kept * TILE, scaled, 0.0).astype(jnp.bfloat16)


def stage_kernel(axis, device_ref, far, near, sem):
    half = near.shape[axis]
    ours = pl.ds(pl.multiple_of((device_ref[0] & 1) * half, half), half)
    copy = pltpu.make_async_copy(far.at[(slice(None),) * axis + (ours,)], near, sem)
    copy.start()
    copy.wait()


def stage(device, weight, axis):
    shape = tuple(size // 2 if at == axis else size for at, size in enumerate(weight.shape))
    return pl.pallas_call(
        functools.partial(stage_kernel, axis),
        in_specs=[SCALARS, FAR],
        out_specs=ON_CHIP,
        out_shape=jax.ShapeDtypeStruct(shape, weight.dtype),
        scratch_shapes=[pltpu.SemaphoreType.DMA],
        compiler_params=params(48),
        cost_estimate=cost(0, 2 * weight.size),
        name="stage",
    )(device, weight)


def begin_kernel(layout, chips, device_ref, length_far, gain_far, key_w_ref, value_far, queries_far, own_far,
                 crossed_ref, plan, gain_ref, value_w_ref, keys_ref, values_ref, own_q_ref, given_q_ref,
                 length_ref, own_ref, raw, rows, sems):
    device = device_ref[0]
    half = value_w_ref.shape[1]
    ours = pl.ds(pl.multiple_of((device & 1) * half, half), half)
    theirs = pl.ds(pl.multiple_of((1 - (device & 1)) * half, half), half)
    moves = (
        (length_far, length_ref),
        (own_far, own_ref),
        (gain_far, gain_ref),
        (value_far.at[:, ours], value_w_ref),
        (queries_far.at[:, ours], own_q_ref),
        (queries_far.at[:, theirs], given_q_ref),
    )
    copies = [
        pltpu.make_async_copy(source, target, sems.at[index])
        for index, (source, target) in enumerate(moves)
    ]
    for copy in copies:
        copy.start()
    copies[0].wait()
    layout.write(plan, device, length_ref, chips)
    copies[1].wait()
    _, kept = keep_valid(layout, plan, 0, [own_ref, crossed_ref], raw)
    copies[2].wait()
    number = raw.shape[0]
    normalize(raw, rows, gain_ref, kept, number)
    for weight_ref, out_ref in ((key_w_ref, keys_ref), (value_w_ref, values_ref)):
        if weight_ref is value_w_ref:
            for copy in copies[3:]:
                copy.wait()
        for left in range(0, half, WIDE):
            columns = slice(left, min(left + WIDE, half))
            out_ref[:number, columns] = jnp.dot(
                rows[...], weight_ref[:, columns], preferred_element_type=jnp.float32
            ).astype(jnp.bfloat16)


def begin(layout, chips, device, passage_length, gain, key_w, value_weight, queries, own, crossed, held_rows):
    width, half = key_w.shape
    held = jax.ShapeDtypeStruct((held_rows, half), jnp.bfloat16)
    query_half = jax.ShapeDtypeStruct((queries.shape[0], half), queries.dtype)
    return pl.pallas_call(
        functools.partial(begin_kernel, layout, chips),
        in_specs=[SCALARS, FAR, FAR, ON_CHIP, FAR, FAR, FAR, ON_CHIP],
        out_specs=[SCALARS] + [ON_CHIP] * 6,
        out_shape=[
            jax.ShapeDtypeStruct((layout.size,), jnp.int32),
            jax.ShapeDtypeStruct(gain.shape, gain.dtype),
            jax.ShapeDtypeStruct(key_w.shape, key_w.dtype),
            held, held, query_half, query_half,
        ],
        scratch_shapes=[
            pltpu.SMEM(passage_length.shape, jnp.int32),
            pltpu.VMEM(own.shape, own.dtype),
            pltpu.VMEM((2 * own.shape[0], width), jnp.bfloat16),
            pltpu.VMEM((2 * own.shape[0], width), jnp.bfloat16),
            pltpu.SemaphoreType.DMA((6,)),
        ],
        compiler_params=params(36),
        cost_estimate=cost(8 * own.shape[0] * width * half, 8 * width * half),
        name="begin",
    )(device, passage_length, gain, key_w, value_weight, queries, own, crossed)


def project_kernel(layout, first, count, cases, stages, plan, gain_ref, key_w_ref, value_w_ref, *refs):
    piece_refs = refs[:count]
    if stages:
        out_far, out_w_ref, sem = refs[count], refs[-4], refs[-1]
        refs = refs[:-4] + refs[-3:-1]
        half = out_w_ref.shape[0]
        ours = pl.ds(pl.multiple_of(layout.core(plan) * half, half), half)
        staging = pltpu.make_async_copy(out_far.at[ours, :], out_w_ref, sem)
        staging.start()
    keys_ref, values_ref, raw, rows = refs[-4:]
    begin_tile, kept = keep_valid(layout, plan, first, piece_refs, raw)
    start = pl.multiple_of(begin_tile * TILE, TILE)
    width = key_w_ref.shape[1]

    def project(number):
        normalize(raw, rows, gain_ref, kept, number)
        for left in range(0, width, WIDE):
            columns = slice(left, min(left + WIDE, width))
            for weight_ref, out_ref in ((key_w_ref, keys_ref), (value_w_ref, values_ref)):
                out_ref[pl.ds(start, number), columns] = jnp.dot(
                    rows[:number, :], weight_ref[:, columns], preferred_element_type=jnp.float32
                ).astype(jnp.bfloat16)

    low = 0
    for number in cases:
        pl.when((kept * TILE > low) & (kept * TILE <= number))(functools.partial(project, number))
        low = number
    if stages:
        staging.wait()


def project(layout, first, plan, gain, key_w, value_w, pieces, held, out_weight=None):
    rows_now = len(pieces) * layout.rows_piece
    width, half = key_w.shape
    cases = sorted({-(-rows_now * part // 3 // TILE) * TILE for part in (2, 3)})
    stages = out_weight is not None
    shapes = [jax.ShapeDtypeStruct(held[0].shape, jnp.bfloat16)] * 2
    if stages:
        shapes.append(jax.ShapeDtypeStruct((half, out_weight.shape[1]), out_weight.dtype))
    at = 4 + len(pieces) + stages
    return pl.pallas_call(
        functools.partial(project_kernel, layout, first, len(pieces), cases, stages),
        in_specs=[SCALARS] + [ON_CHIP] * (3 + len(pieces)) + [FAR] * stages + [ON_CHIP] * 2,
        out_specs=[ON_CHIP] * len(shapes),
        out_shape=shapes,
        scratch_shapes=[pltpu.VMEM((rows_now, width), jnp.bfloat16)] * 2 + [pltpu.SemaphoreType.DMA] * stages,
        input_output_aliases={at: 0, at + 1: 1},
        compiler_params=params(28 if stages else 16),
        cost_estimate=cost(4 * rows_now * width * half, 4 * width * half),
        name="project",
    )(plan, gain, key_w, value_w, *pieces, *([out_weight] if stages else []), *held)


def attend_kernel(layout, cases, plan, own_q_ref, other_q_ref, keys_ref, values_ref, out_w_ref,
                  own_ref, other_ref, mask):
    half, inner = own_q_ref.shape
    heads = inner // DK
    kept = layout.total(plan)
    row = lax.broadcasted_iota(jnp.int32, mask.shape, 0)
    valid = row < kept * TILE
    for passage in range(layout.passages):
        begin = layout.partial(plan, passage)
        end = ((begin + TILE - 1) >> (TILE.bit_length() - 1)) * TILE
        valid = valid & ((begin < 0) | (row < begin) | (row >= end))
    first_column = lax.broadcasted_iota(jnp.int32, mask.shape, 1) == 0
    mask[...] = jnp.where(first_column & ~valid, LOWEST, 0.0).astype(jnp.bfloat16)

    def attend(number):
        def clear(tile, carry):
            at = pl.ds(pl.multiple_of(tile * TILE, TILE), TILE)
            keys_ref[at, :] = jnp.zeros((TILE, inner), jnp.bfloat16)
            values_ref[at, :] = jnp.zeros((TILE, inner), jnp.bfloat16)
            return carry

        lax.fori_loop(kept, number // TILE, clear, 0)
        ones = jnp.where(
            lax.broadcasted_iota(jnp.int32, (2 * half, DK), 1) == 0, 1.0, 0.0
        ).astype(jnp.bfloat16)

        def scores_of(head):
            here = slice(head * DK, (head + 1) * DK)
            query_rows = jnp.concatenate([own_q_ref[:, here], other_q_ref[:, here]], axis=0)
            return lax.dot_general(
                jnp.concatenate([query_rows, ones], axis=1),
                jnp.concatenate([keys_ref[:number, here], mask[:number, :]], axis=1),
                (((1,), (1,)), ((), ())), preferred_element_type=jnp.float32,
            )

        def weigh(scores):
            expo = jnp.exp(scores - jnp.max(scores, axis=-1, keepdims=True))
            return expo.astype(jnp.bfloat16), jnp.sum(expo, axis=-1, keepdims=True)

        def mix(head, weights, denom):
            mixed = jnp.dot(
                weights, values_ref[:number, head * DK:(head + 1) * DK],
                preferred_element_type=jnp.float32,
            )
            return (mixed * (1.0 / denom)).astype(jnp.bfloat16)

        attended, scores, weighed = [], scores_of(0), None
        for head in range(heads):
            ahead = scores_of(head + 1) if head + 1 < heads else None
            weighing = weigh(scores)
            if weighed is not None:
                attended.append(mix(head - 1, *weighed))
            scores, weighed = ahead, weighing
        attended.append(mix(heads - 1, *weighed))
        product = jnp.dot(
            jnp.concatenate(attended, axis=1), out_w_ref[...], preferred_element_type=jnp.float32
        )
        own_ref[...] = product[:half, :].astype(jnp.bfloat16)
        other_ref[...] = product[half:, :].astype(jnp.bfloat16)

    low = 0
    for number in cases:
        pl.when((kept * TILE > low) & (kept * TILE <= number))(functools.partial(attend, number))
        low = number


def attend(layout, plan, own_q, other_q, keys, values, out_w):
    rows_here, half = own_q.shape
    width = out_w.shape[1]
    enc_rows = layout.tiles * TILE
    cases = [enc_rows * 2 // 3 // 64 * 64, enc_rows]
    return pl.pallas_call(
        functools.partial(attend_kernel, layout, cases),
        in_specs=[SCALARS] + [ON_CHIP] * 5,
        out_specs=[ON_CHIP] * 2,
        out_shape=[jax.ShapeDtypeStruct((rows_here, width), jnp.bfloat16)] * 2,
        scratch_shapes=[pltpu.VMEM((enc_rows, DK), jnp.bfloat16)],
        compiler_params=params(24),
        cost_estimate=cost(4 * rows_here * (2 * enc_rows + width) * half, 2 * half * width),
        name="attend",
    )(plan, own_q, other_q, keys, values, out_w)


def on_device(number, queries, passages, enc_gain, key_weight, value_weight, out_weight, passage_length):
    rows_piece = passages.shape[0]
    heads_axis = lax.axis_size("heads")
    chips = number // 2
    cycle = chip_cycle(chips)
    place = {chip: index for index, chip in enumerate(cycle)}
    other_core = [(device, device ^ 1) for device in range(number)]

    def hop(by, crossed=0):
        return [
            (2 * chip + core, 2 * cycle[(place[chip] + by) % chips] + (core ^ crossed))
            for chip in range(chips)
            for core in range(2)
        ]

    def cross(piece):
        return lax.ppermute(piece, "rows", other_core)

    near = [1, 2] if chips > 4 else [1]
    reach = [near] + [[by] for by in range(near[-1] + 1, chips // 2 + 1)]
    rounds = []
    for distances in reach:
        if 2 * distances[0] == chips:
            rounds.append([(-distances[0], 0), (distances[0], 1)])
        else:
            sources = [(sign * by, 0) for by in distances for sign in (-1, 1)]
            rounds.append(sources + [(offset, 1) for offset, _ in sources])
    order = [(0, 0), (0, 1)] + [source for sources in rounds for source in sources]
    layout = Plan(order, rows_piece, passage_length.shape[0])

    device = lax.axis_index("rows").reshape(1)
    held_rows = number * rows_piece + 4 * rows_piece
    key_w = stage(device, key_weight, 1)
    plan, gain, value_w, *held, own_q, given_q = begin(
        layout, chips, device, passage_length, enc_gain, key_w, value_weight,
        queries, passages, cross(passages), held_rows,
    )
    other_q = cross(given_q)

    arrived = [lax.ppermute(passages, "rows", hop(-offset)) for offset, crossed in rounds[0] if not crossed]
    staged_by = max(0, len(rounds) - 2)
    first, out_w = 2, None
    for index, (sources, later) in enumerate(zip(rounds, rounds[1:] + [None])):
        *pieces, keys, values = lax.optimization_barrier((*arrived, *held))
        held = [keys, values]
        if later:
            ahead, behind = pieces[-2:]
            last_two = len(later) == 2
            arrived = [
                lax.ppermute(ahead, "rows", hop(1)),
                lax.ppermute(behind, "rows", hop(-1, 1 if last_two else 0)),
            ]
        if len(sources) > 2:
            pieces = pieces + [cross(piece) for piece in pieces]
        *held, last = project(
            layout, first, plan, gain, key_w, value_w, pieces, held, out_weight if index == staged_by else None
        )
        if index == staged_by:
            out_w = last
        else:
            held.append(last)
        first += len(pieces)
    keys, values = held

    own, other = attend(layout, plan, own_q, other_q, keys, values, out_w)
    share = (own.astype(jnp.float32) + cross(other).astype(jnp.float32)).astype(jnp.bfloat16)
    by = 1
    while by < heads_axis:
        turn = [(place, place ^ by) for place in range(heads_axis)]
        given = lax.ppermute(share, "heads", turn)
        share = (share.astype(jnp.float32) + given.astype(jnp.float32)).astype(jnp.bfloat16)
        by *= 2
    return share


def solution(mesh):
    return jax.shard_map(
        functools.partial(on_device, mesh.shape["rows"]),
        mesh=mesh,
        in_specs=(
            P(("groups", "rows"), "heads"),
            P(("groups", "rows"), None),
            P(),
            P(None, "heads"),
            P(None, "heads"),
            P("heads", None),
            P("groups"),
        ),
        out_specs=P(("groups", "rows"), None),
        check_vma=False,
    )
```

```python
import functools

import jax
import jax.numpy as jnp
from jax import lax
from jax.experimental import pallas as pl
from jax.experimental.pallas import tpu as pltpu
from jax.sharding import PartitionSpec as P

DK = 128
PASS_LEN = 256
LOWEST = -1e30
TILE = 16
WIDE = 1024
ON_CHIP = pl.BlockSpec(memory_space=pltpu.VMEM)
SCALARS = pl.BlockSpec(memory_space=pltpu.SMEM)
FAR = pl.BlockSpec(memory_space=pltpu.HBM)


def params(mib):
    return pltpu.CompilerParams(vmem_limit_bytes=mib * 1024 * 1024)


def cost(flops, moved, exps=0):
    return pl.CostEstimate(flops=flops, bytes_accessed=moved, transcendentals=exps)


def chip_cycle(chips):
    up = list(range(0, chips, 2))
    return up + [chip for chip in range(chips - 1, -1, -1) if chip % 2]


def owner_of(device, source, chips):
    offset, crossed = source
    chip, core = device >> 1, device & 1
    place = jnp.where((chip & 1) == 0, chip >> 1, chips - ((chip + 1) >> 1)) + offset
    place = jnp.where(place < 0, place + chips, jnp.where(place >= chips, place - chips, place))
    chip = jnp.where(place < (chips + 1) >> 1, place << 1, ((chips - place) << 1) - 1)
    return (chip << 1) + (core ^ crossed)


class Plan:
    def __init__(self, order, rows_piece, passages):
        self.order, self.per_piece = order, rows_piece // TILE
        self.rows_piece, self.passages = rows_piece, passages
        self.tiles = len(order) * self.per_piece
        self.size = 2 * self.tiles + 2 + passages

    def write(self, plan, device, length_ref, chips):
        shift = PASS_LEN.bit_length() - 1
        for passage in range(self.passages):
            plan[2 * self.tiles + 2 + passage] = -1
        kept = jnp.int32(0)
        for index, source in enumerate(self.order):
            first = owner_of(device, source, chips) * self.rows_piece
            for tile in range(index * self.per_piece, (index + 1) * self.per_piece):
                row = first + (tile - index * self.per_piece) * TILE
                passage = row >> shift
                here = length_ref[passage] - (row & (PASS_LEN - 1))
                plan[tile] = here
                plan[self.tiles + tile] = kept

                @pl.when((here > 0) & (here < TILE))
                def _(kept=kept, here=here, passage=passage):
                    plan[2 * self.tiles + 2 + passage] = kept * TILE + here

                kept = kept + (here > 0).astype(jnp.int32)
        plan[2 * self.tiles] = kept
        plan[2 * self.tiles + 1] = device & 1

    def here(self, plan, tile):
        return plan[tile]

    def place(self, plan, tile):
        return plan[self.tiles + tile]

    def total(self, plan):
        return plan[2 * self.tiles]

    def core(self, plan):
        return plan[2 * self.tiles + 1]

    def partial(self, plan, passage):
        return plan[2 * self.tiles + 2 + passage]


def keep_valid(layout, plan, first, piece_refs, raw):
    begin = layout.place(plan, first * layout.per_piece)
    after = (first + len(piece_refs)) * layout.per_piece
    for index, piece_ref in enumerate(piece_refs):
        for tile in range(layout.per_piece):
            at = (first + index) * layout.per_piece + tile

            @pl.when(layout.here(plan, at) > 0)
            def _(at=at, tile=tile, piece_ref=piece_ref):
                row = pl.multiple_of((layout.place(plan, at) - begin) * TILE, TILE)
                raw[pl.ds(row, TILE), :] = piece_ref[tile * TILE:(tile + 1) * TILE, :]

    end = layout.place(plan, after) if after < layout.tiles else layout.total(plan)
    return begin, end - begin


def normalize(raw, rows, gain_ref, kept, number):
    wide = raw[:number, :].astype(jnp.float32)
    mean_square = jnp.mean(wide * wide, axis=-1, keepdims=True)
    scaled = wide * lax.rsqrt(mean_square + 1e-06) * gain_ref[...].astype(jnp.float32).reshape(1, -1)
    row = lax.broadcasted_iota(jnp.int32, scaled.shape, 0)
    rows[:number, :] = jnp.where(row < kept * TILE, scaled, 0.0).astype(jnp.bfloat16)


def stage_kernel(axis, device_ref, far, near, sem):
    half = near.shape[axis]
    ours = pl.ds(pl.multiple_of((device_ref[0] & 1) * half, half), half)
    copy = pltpu.make_async_copy(far.at[(slice(None),) * axis + (ours,)], near, sem)
    copy.start()
    copy.wait()


def stage(device, weight, axis):
    shape = tuple(size // 2 if at == axis else size for at, size in enumerate(weight.shape))
    return pl.pallas_call(
        functools.partial(stage_kernel, axis),
        in_specs=[SCALARS, FAR],
        out_specs=ON_CHIP,
        out_shape=jax.ShapeDtypeStruct(shape, weight.dtype),
        scratch_shapes=[pltpu.SemaphoreType.DMA],
        compiler_params=params(48),
        cost_estimate=cost(0, 2 * weight.size),
        name="stage",
    )(device, weight)


def write_mask(layout, plan, mask_ref):
    row = lax.broadcasted_iota(jnp.int32, mask_ref.shape, 0)
    valid = row < layout.total(plan) * TILE
    for passage in range(layout.passages):
        begin = layout.partial(plan, passage)
        end = ((begin + TILE - 1) >> (TILE.bit_length() - 1)) * TILE
        valid = valid & ((begin < 0) | (row < begin) | (row >= end))
    first_column = lax.broadcasted_iota(jnp.int32, mask_ref.shape, 1) == 0
    mask_ref[...] = jnp.where(first_column & ~valid, LOWEST, 0.0).astype(jnp.bfloat16)


def begin_kernel(layout, chips, device_ref, length_far, gain_far, key_w_ref, value_far, queries_far, own_far,
                 crossed_ref, plan, gain_ref, value_w_ref, keys_ref, values_ref, own_q_ref, given_q_ref, mask_ref,
                 length_ref, own_ref, raw, rows, sems):
    device = device_ref[0]
    half = value_w_ref.shape[1]
    ours = pl.ds(pl.multiple_of((device & 1) * half, half), half)
    theirs = pl.ds(pl.multiple_of((1 - (device & 1)) * half, half), half)
    moves = (
        (length_far, length_ref),
        (own_far, own_ref),
        (gain_far, gain_ref),
        (value_far.at[:, ours], value_w_ref),
        (queries_far.at[:, ours], own_q_ref),
        (queries_far.at[:, theirs], given_q_ref),
    )
    copies = [
        pltpu.make_async_copy(source, target, sems.at[index])
        for index, (source, target) in enumerate(moves)
    ]
    for copy in copies:
        copy.start()
    copies[0].wait()
    layout.write(plan, device, length_ref, chips)
    copies[1].wait()
    _, kept = keep_valid(layout, plan, 0, [own_ref, crossed_ref], raw)
    copies[2].wait()
    number = raw.shape[0]
    normalize(raw, rows, gain_ref, kept, number)
    for weight_ref, out_ref in ((key_w_ref, keys_ref), (value_w_ref, values_ref)):
        if weight_ref is value_w_ref:
            write_mask(layout, plan, mask_ref)
            for copy in copies[3:]:
                copy.wait()
        for left in range(0, half, WIDE):
            columns = slice(left, min(left + WIDE, half))
            out_ref[:number, columns] = jnp.dot(
                rows[...], weight_ref[:, columns], preferred_element_type=jnp.float32
            ).astype(jnp.bfloat16)


def begin(layout, chips, device, passage_length, gain, key_w, value_weight, queries, own, crossed, held_rows):
    width, half = key_w.shape
    held = jax.ShapeDtypeStruct((held_rows, half), jnp.bfloat16)
    query_half = jax.ShapeDtypeStruct((queries.shape[0], half), queries.dtype)
    return pl.pallas_call(
        functools.partial(begin_kernel, layout, chips),
        in_specs=[SCALARS, FAR, FAR, ON_CHIP, FAR, FAR, FAR, ON_CHIP],
        out_specs=[SCALARS] + [ON_CHIP] * 7,
        out_shape=[
            jax.ShapeDtypeStruct((layout.size,), jnp.int32),
            jax.ShapeDtypeStruct(gain.shape, gain.dtype),
            jax.ShapeDtypeStruct(key_w.shape, key_w.dtype),
            held, held, query_half, query_half,
            jax.ShapeDtypeStruct((layout.tiles * TILE, DK), jnp.bfloat16),
        ],
        scratch_shapes=[
            pltpu.SMEM(passage_length.shape, jnp.int32),
            pltpu.VMEM(own.shape, own.dtype),
            pltpu.VMEM((2 * own.shape[0], width), jnp.bfloat16),
            pltpu.VMEM((2 * own.shape[0], width), jnp.bfloat16),
            pltpu.SemaphoreType.DMA((6,)),
        ],
        compiler_params=params(36),
        cost_estimate=cost(8 * own.shape[0] * width * half, 8 * width * half),
        name="begin",
    )(device, passage_length, gain, key_w, value_weight, queries, own, crossed)


def append(layout, first, cases, plan, piece_refs, gain_ref, key_w_ref, value_w_ref, keys_ref, values_ref, raw, rows):
    begin_tile, kept = keep_valid(layout, plan, first, piece_refs, raw)
    start = pl.multiple_of(begin_tile * TILE, TILE)
    width = key_w_ref.shape[1]

    def project(number):
        normalize(raw, rows, gain_ref, kept, number)
        for left in range(0, width, WIDE):
            columns = slice(left, min(left + WIDE, width))
            for weight_ref, out_ref in ((key_w_ref, keys_ref), (value_w_ref, values_ref)):
                out_ref[pl.ds(start, number), columns] = jnp.dot(
                    rows[:number, :], weight_ref[:, columns], preferred_element_type=jnp.float32
                ).astype(jnp.bfloat16)

    low = 0
    for number in cases:
        pl.when((kept * TILE > low) & (kept * TILE <= number))(functools.partial(project, number))
        low = number


def cases_of(rows_now):
    return list(range(rows_now, rows_now // 3, -64))[::-1]


def project_kernel(layout, first, count, cases, stages, plan, gain_ref, key_w_ref, value_w_ref, *refs):
    piece_refs = refs[:count]
    if stages:
        out_far, out_w_ref, sem = refs[count], refs[-4], refs[-1]
        refs = refs[:-4] + refs[-3:-1]
        half = out_w_ref.shape[0]
        ours = pl.ds(pl.multiple_of(layout.core(plan) * half, half), half)
        staging = pltpu.make_async_copy(out_far.at[ours, :], out_w_ref, sem)
        staging.start()
    keys_ref, values_ref, raw, rows = refs[-4:]
    append(layout, first, cases, plan, piece_refs, gain_ref, key_w_ref, value_w_ref, keys_ref, values_ref, raw, rows)
    if stages:
        staging.wait()


def project(layout, first, plan, gain, key_w, value_w, pieces, held, out_weight=None):
    rows_now = len(pieces) * layout.rows_piece
    width, half = key_w.shape
    stages = out_weight is not None
    shapes = [jax.ShapeDtypeStruct(held[0].shape, jnp.bfloat16)] * 2
    if stages:
        shapes.append(jax.ShapeDtypeStruct((half, out_weight.shape[1]), out_weight.dtype))
    at = 4 + len(pieces) + stages
    return pl.pallas_call(
        functools.partial(project_kernel, layout, first, len(pieces), cases_of(rows_now), stages),
        in_specs=[SCALARS] + [ON_CHIP] * (3 + len(pieces)) + [FAR] * stages + [ON_CHIP] * 2,
        out_specs=[ON_CHIP] * len(shapes),
        out_shape=shapes,
        scratch_shapes=[pltpu.VMEM((rows_now, width), jnp.bfloat16)] * 2 + [pltpu.SemaphoreType.DMA] * stages,
        input_output_aliases={at: 0, at + 1: 1},
        compiler_params=params(28 if stages else 16),
        cost_estimate=cost(4 * rows_now * width * half, 4 * width * half),
        name="project",
    )(plan, gain, key_w, value_w, *pieces, *([out_weight] if stages else []), *held)


def attend_kernel(layout, first, count, cases, plan, gain_ref, key_w_ref, value_w_ref, mask, own_q_ref, other_q_ref,
                  out_w_ref, *refs):
    piece_refs = refs[:count]
    own_ref, other_ref, keys_ref, values_ref, raw, rows = refs[count + 2:]
    append(layout, first, cases_of(raw.shape[0]), plan, piece_refs, gain_ref, key_w_ref, value_w_ref,
           keys_ref, values_ref, raw, rows)
    half, inner = own_q_ref.shape
    heads = inner // DK
    kept = layout.total(plan)

    def attend(number):
        def clear(tile, carry):
            at = pl.ds(pl.multiple_of(tile * TILE, TILE), TILE)
            keys_ref[at, :] = jnp.zeros((TILE, inner), jnp.bfloat16)
            values_ref[at, :] = jnp.zeros((TILE, inner), jnp.bfloat16)
            return carry

        lax.fori_loop(kept, number // TILE, clear, 0)
        ones = jnp.where(
            lax.broadcasted_iota(jnp.int32, (2 * half, DK), 1) == 0, 1.0, 0.0
        ).astype(jnp.bfloat16)

        def scores_of(head):
            here = slice(head * DK, (head + 1) * DK)
            query_rows = jnp.concatenate([own_q_ref[:, here], other_q_ref[:, here]], axis=0)
            return lax.dot_general(
                jnp.concatenate([query_rows, ones], axis=1),
                jnp.concatenate([keys_ref[:number, here], mask[:number, :]], axis=1),
                (((1,), (1,)), ((), ())), preferred_element_type=jnp.float32,
            )

        def weigh(scores):
            expo = jnp.exp(scores - jnp.max(scores, axis=-1, keepdims=True))
            return expo.astype(jnp.bfloat16), jnp.sum(expo, axis=-1, keepdims=True)

        def mix(head, weights, denom):
            mixed = jnp.dot(
                weights, values_ref[:number, head * DK:(head + 1) * DK],
                preferred_element_type=jnp.float32,
            )
            return (mixed * (1.0 / denom)).astype(jnp.bfloat16)

        attended, scores, weighed = [], scores_of(0), None
        for head in range(heads):
            ahead = scores_of(head + 1) if head + 1 < heads else None
            weighing = weigh(scores)
            if weighed is not None:
                attended.append(mix(head - 1, *weighed))
            scores, weighed = ahead, weighing
        attended.append(mix(heads - 1, *weighed))
        product = jnp.dot(
            jnp.concatenate(attended, axis=1), out_w_ref[...], preferred_element_type=jnp.float32
        )
        own_ref[...] = product[:half, :].astype(jnp.bfloat16)
        other_ref[...] = product[half:, :].astype(jnp.bfloat16)

    low = 0
    for number in cases:
        pl.when((kept * TILE > low) & (kept * TILE <= number))(functools.partial(attend, number))
        low = number


def attend(layout, first, plan, gain, key_w, value_w, mask, own_q, other_q, out_w, pieces, held):
    rows_here, half = own_q.shape
    width = out_w.shape[1]
    enc_rows = layout.tiles * TILE
    cases = [enc_rows * 2 // 3 // 64 * 64, enc_rows]
    result = jax.ShapeDtypeStruct((rows_here, width), jnp.bfloat16)
    kept = jax.ShapeDtypeStruct(held[0].shape, jnp.bfloat16)
    at = 8 + len(pieces)
    own, other, _, _ = pl.pallas_call(
        functools.partial(attend_kernel, layout, first, len(pieces), cases),
        in_specs=[SCALARS] + [ON_CHIP] * (at + 1),
        out_specs=[ON_CHIP] * 4,
        out_shape=[result, result, kept, kept],
        scratch_shapes=[pltpu.VMEM((len(pieces) * layout.rows_piece, width), jnp.bfloat16)] * 2,
        input_output_aliases={at: 2, at + 1: 3},
        compiler_params=params(24),
        cost_estimate=cost(4 * rows_here * (2 * enc_rows + width) * half, 2 * half * width),
        name="attend",
    )(plan, gain, key_w, value_w, mask, own_q, other_q, out_w, *pieces, *held)
    return own, other


def on_device(number, queries, passages, enc_gain, key_weight, value_weight, out_weight, passage_length):
    rows_piece = passages.shape[0]
    heads_axis = lax.axis_size("heads")
    chips = number // 2
    cycle = chip_cycle(chips)
    place = {chip: index for index, chip in enumerate(cycle)}
    other_core = [(device, device ^ 1) for device in range(number)]

    def hop(by, crossed=0):
        return [
            (2 * chip + core, 2 * cycle[(place[chip] + by) % chips] + (core ^ crossed))
            for chip in range(chips)
            for core in range(2)
        ]

    def cross(piece):
        return lax.ppermute(piece, "rows", other_core)

    rounds = []
    for distance in range(1, chips // 2 + 1):
        if 2 * distance == chips:
            rounds.append([(-distance, 0), (distance, 1)])
        else:
            rounds.append([(-distance, 0), (distance, 0), (-distance, 1), (distance, 1)])
    order = [(0, 0), (0, 1)] + [source for sources in rounds for source in sources]
    layout = Plan(order, rows_piece, passage_length.shape[0])

    device = lax.axis_index("rows").reshape(1)
    held_rows = number * rows_piece
    crossed = cross(passages)
    ahead = behind = passages
    first, waiting, held, out_w = 2, [], [], None
    for index, sources in enumerate(rounds):
        ahead = lax.ppermute(ahead, "rows", hop(1))
        behind = lax.ppermute(behind, "rows", hop(-1, 1 if len(sources) == 2 else 0))
        if index == 0:
            key_w = stage(device, key_weight, 1)
            ahead, behind, key_w = lax.optimization_barrier((ahead, behind, key_w))
        if index == min(1, len(rounds) - 1):
            plan, gain, value_w, keys, values, own_q, given_q, mask = begin(
                layout, chips, device, passage_length, enc_gain, key_w, value_weight,
                queries, passages, crossed, held_rows,
            )
            held = [keys, values]
        elif index > 1:
            last = index == len(rounds) - 1
            now = len(waiting) if last else 6
            *held, staged = project(
                layout, first, plan, gain, key_w, value_w, waiting[:now], held, out_weight if last else None
            )
            if last:
                out_w = staged
            else:
                held.append(staged)
            first, waiting = first + now, waiting[now:]
        ahead, behind, *held = lax.optimization_barrier((ahead, behind, *held))
        waiting = waiting + ([ahead, behind] if len(sources) == 2 else [ahead, behind, cross(ahead), cross(behind)])
    if out_w is None:
        out_w = stage(device, out_weight, 0)
    other_q = cross(given_q)

    own, other = attend(
        layout, first, plan, gain, key_w, value_w, mask, own_q, other_q, out_w, waiting, held
    )
    share = (own.astype(jnp.float32) + cross(other).astype(jnp.float32)).astype(jnp.bfloat16)
    by = 1
    while by < heads_axis:
        turn = [(place, place ^ by) for place in range(heads_axis)]
        given = lax.ppermute(share, "heads", turn)
        share = (share.astype(jnp.float32) + given.astype(jnp.float32)).astype(jnp.bfloat16)
        by *= 2
    return share


def solution(mesh):
    return jax.shard_map(
        functools.partial(on_device, mesh.shape["rows"]),
        mesh=mesh,
        in_specs=(
            P(("groups", "rows"), "heads"),
            P(("groups", "rows"), None),
            P(),
            P(None, "heads"),
            P(None, "heads"),
            P("heads", None),
            P("groups"),
        ),
        out_specs=P(("groups", "rows"), None),
        check_vma=False,
    )
```

```python
import functools

import jax
import jax.numpy as jnp
from jax import lax
from jax.experimental import pallas as pl
from jax.experimental.pallas import tpu as pltpu
from jax.sharding import PartitionSpec as P

DK = 128
PASS_LEN = 256
LOWEST = -1e30
TILE = 16
TAIL_PARTS = 2
WIDE = 1024
ON_CHIP = pl.BlockSpec(memory_space=pltpu.VMEM)
SCALARS = pl.BlockSpec(memory_space=pltpu.SMEM)
FAR = pl.BlockSpec(memory_space=pltpu.HBM)


def params(mib):
    return pltpu.CompilerParams(vmem_limit_bytes=mib * 1024 * 1024)


def cost(flops, moved, exps=0):
    return pl.CostEstimate(flops=flops, bytes_accessed=moved, transcendentals=exps)


def chip_cycle(chips):
    up = list(range(0, chips, 2))
    return up + [chip for chip in range(chips - 1, -1, -1) if chip % 2]


def owner_of(device, source, chips):
    offset, crossed = source
    chip, core = device >> 1, device & 1
    place = jnp.where((chip & 1) == 0, chip >> 1, chips - ((chip + 1) >> 1)) + offset
    place = jnp.where(place < 0, place + chips, jnp.where(place >= chips, place - chips, place))
    chip = jnp.where(place < (chips + 1) >> 1, place << 1, ((chips - place) << 1) - 1)
    return (chip << 1) + (core ^ crossed)


class Plan:
    def __init__(self, order, rows_piece, passages):
        self.order, self.per_piece = order, rows_piece // TILE
        self.rows_piece, self.passages = rows_piece, passages
        self.tiles = len(order) * self.per_piece
        self.size = 2 * self.tiles + 2 + passages

    def write(self, plan, device, length_ref, chips):
        shift = PASS_LEN.bit_length() - 1
        for passage in range(self.passages):
            plan[2 * self.tiles + 2 + passage] = -1
        kept = jnp.int32(0)
        for index, source in enumerate(self.order):
            first = owner_of(device, source, chips) * self.rows_piece
            for tile in range(index * self.per_piece, (index + 1) * self.per_piece):
                row = first + (tile - index * self.per_piece) * TILE
                passage = row >> shift
                here = length_ref[passage] - (row & (PASS_LEN - 1))
                plan[tile] = here
                plan[self.tiles + tile] = kept

                @pl.when((here > 0) & (here < TILE))
                def _(kept=kept, here=here, passage=passage):
                    plan[2 * self.tiles + 2 + passage] = kept * TILE + here

                kept = kept + (here > 0).astype(jnp.int32)
        plan[2 * self.tiles] = kept
        plan[2 * self.tiles + 1] = device & 1

    def here(self, plan, tile):
        return plan[tile]

    def place(self, plan, tile):
        return plan[self.tiles + tile]

    def total(self, plan):
        return plan[2 * self.tiles]

    def core(self, plan):
        return plan[2 * self.tiles + 1]

    def partial(self, plan, passage):
        return plan[2 * self.tiles + 2 + passage]


def keep_valid(layout, plan, first, piece_refs, raw):
    begin = layout.place(plan, first * layout.per_piece)
    after = (first + len(piece_refs)) * layout.per_piece
    for index, piece_ref in enumerate(piece_refs):
        for tile in range(layout.per_piece):
            at = (first + index) * layout.per_piece + tile

            @pl.when(layout.here(plan, at) > 0)
            def _(at=at, tile=tile, piece_ref=piece_ref):
                row = pl.multiple_of((layout.place(plan, at) - begin) * TILE, TILE)
                raw[pl.ds(row, TILE), :] = piece_ref[tile * TILE:(tile + 1) * TILE, :]

    end = layout.place(plan, after) if after < layout.tiles else layout.total(plan)
    return begin, end - begin


def normalize(raw, rows, gain_ref, kept, number):
    wide = raw[:number, :].astype(jnp.float32)
    mean_square = jnp.mean(wide * wide, axis=-1, keepdims=True)
    scaled = wide * lax.rsqrt(mean_square + 1e-06) * gain_ref[...].astype(jnp.float32).reshape(1, -1)
    row = lax.broadcasted_iota(jnp.int32, scaled.shape, 0)
    rows[:number, :] = jnp.where(row < kept * TILE, scaled, 0.0).astype(jnp.bfloat16)


def stage_kernel(axis, device_ref, far, near, sem):
    half = near.shape[axis]
    ours = pl.ds(pl.multiple_of((device_ref[0] & 1) * half, half), half)
    copy = pltpu.make_async_copy(far.at[(slice(None),) * axis + (ours,)], near, sem)
    copy.start()
    copy.wait()


def stage(device, weight, axis):
    shape = tuple(size // 2 if at == axis else size for at, size in enumerate(weight.shape))
    return pl.pallas_call(
        functools.partial(stage_kernel, axis),
        in_specs=[SCALARS, FAR],
        out_specs=ON_CHIP,
        out_shape=jax.ShapeDtypeStruct(shape, weight.dtype),
        scratch_shapes=[pltpu.SemaphoreType.DMA],
        compiler_params=params(48),
        cost_estimate=cost(0, 2 * weight.size),
        name="stage",
    )(device, weight)


def write_mask(layout, plan, mask_ref):
    row = lax.broadcasted_iota(jnp.int32, mask_ref.shape, 0)
    valid = row < layout.total(plan) * TILE
    for passage in range(layout.passages):
        begin = layout.partial(plan, passage)
        end = ((begin + TILE - 1) >> (TILE.bit_length() - 1)) * TILE
        valid = valid & ((begin < 0) | (row < begin) | (row >= end))
    first_column = lax.broadcasted_iota(jnp.int32, mask_ref.shape, 1) == 0
    mask_ref[...] = jnp.where(first_column & ~valid, LOWEST, 0.0).astype(jnp.bfloat16)


def begin_kernel(layout, chips, device_ref, length_far, gain_far, key_w_ref, value_far, queries_far, own_far,
                 crossed_ref, plan, gain_ref, value_w_ref, keys_ref, values_ref, own_q_ref, given_q_ref, mask_ref,
                 length_ref, own_ref, raw, rows, sems):
    device = device_ref[0]
    half = value_w_ref.shape[1]
    ours = pl.ds(pl.multiple_of((device & 1) * half, half), half)
    theirs = pl.ds(pl.multiple_of((1 - (device & 1)) * half, half), half)
    moves = (
        (length_far, length_ref),
        (own_far, own_ref),
        (gain_far, gain_ref),
        (value_far.at[:, ours], value_w_ref),
        (queries_far.at[:, ours], own_q_ref),
        (queries_far.at[:, theirs], given_q_ref),
    )
    copies = [
        pltpu.make_async_copy(source, target, sems.at[index])
        for index, (source, target) in enumerate(moves)
    ]
    for copy in copies:
        copy.start()
    copies[0].wait()
    layout.write(plan, device, length_ref, chips)
    copies[1].wait()
    _, kept = keep_valid(layout, plan, 0, [own_ref, crossed_ref], raw)
    copies[2].wait()
    number = raw.shape[0]
    normalize(raw, rows, gain_ref, kept, number)
    for weight_ref, out_ref in ((key_w_ref, keys_ref), (value_w_ref, values_ref)):
        if weight_ref is value_w_ref:
            write_mask(layout, plan, mask_ref)
            for copy in copies[3:]:
                copy.wait()
        for left in range(0, half, WIDE):
            columns = slice(left, min(left + WIDE, half))
            out_ref[:number, columns] = jnp.dot(
                rows[...], weight_ref[:, columns], preferred_element_type=jnp.float32
            ).astype(jnp.bfloat16)


def begin(layout, chips, device, passage_length, gain, key_w, value_weight, queries, own, crossed, held_rows):
    width, half = key_w.shape
    held = jax.ShapeDtypeStruct((held_rows, half), jnp.bfloat16)
    query_half = jax.ShapeDtypeStruct((queries.shape[0], half), queries.dtype)
    return pl.pallas_call(
        functools.partial(begin_kernel, layout, chips),
        in_specs=[SCALARS, FAR, FAR, ON_CHIP, FAR, FAR, FAR, ON_CHIP],
        out_specs=[SCALARS] + [ON_CHIP] * 7,
        out_shape=[
            jax.ShapeDtypeStruct((layout.size,), jnp.int32),
            jax.ShapeDtypeStruct(gain.shape, gain.dtype),
            jax.ShapeDtypeStruct(key_w.shape, key_w.dtype),
            held, held, query_half, query_half,
            jax.ShapeDtypeStruct((layout.tiles * TILE, DK), jnp.bfloat16),
        ],
        scratch_shapes=[
            pltpu.SMEM(passage_length.shape, jnp.int32),
            pltpu.VMEM(own.shape, own.dtype),
            pltpu.VMEM((2 * own.shape[0], width), jnp.bfloat16),
            pltpu.VMEM((2 * own.shape[0], width), jnp.bfloat16),
            pltpu.SemaphoreType.DMA((6,)),
        ],
        compiler_params=params(36),
        cost_estimate=cost(8 * own.shape[0] * width * half, 8 * width * half),
        name="begin",
    )(device, passage_length, gain, key_w, value_weight, queries, own, crossed)


def append(layout, first, cases, plan, piece_refs, gain_ref, key_w_ref, value_w_ref, keys_ref, values_ref, raw, rows):
    begin_tile, kept = keep_valid(layout, plan, first, piece_refs, raw)
    start = pl.multiple_of(begin_tile * TILE, TILE)
    width = key_w_ref.shape[1]

    def project(number):
        normalize(raw, rows, gain_ref, kept, number)
        for left in range(0, width, WIDE):
            columns = slice(left, min(left + WIDE, width))
            for weight_ref, out_ref in ((key_w_ref, keys_ref), (value_w_ref, values_ref)):
                out_ref[pl.ds(start, number), columns] = jnp.dot(
                    rows[:number, :], weight_ref[:, columns], preferred_element_type=jnp.float32
                ).astype(jnp.bfloat16)

    low = 0
    for number in cases:
        pl.when((kept * TILE > low) & (kept * TILE <= number))(functools.partial(project, number))
        low = number


def cases_of(rows_now):
    return list(range(rows_now, rows_now // 3, -64))[::-1]


def project_kernel(layout, first, count, cases, stages, plan, gain_ref, key_w_ref, value_w_ref, *refs):
    piece_refs = refs[:count]
    if stages:
        out_far, out_w_ref, sem = refs[count], refs[-4], refs[-1]
        refs = refs[:-4] + refs[-3:-1]
        half = out_w_ref.shape[0]
        ours = pl.ds(pl.multiple_of(layout.core(plan) * half, half), half)
        staging = pltpu.make_async_copy(out_far.at[ours, :], out_w_ref, sem)
        staging.start()
    keys_ref, values_ref, raw, rows = refs[-4:]
    append(layout, first, cases, plan, piece_refs, gain_ref, key_w_ref, value_w_ref, keys_ref, values_ref, raw, rows)
    if stages:
        staging.wait()


def project(layout, first, plan, gain, key_w, value_w, pieces, held, out_weight=None):
    rows_now = len(pieces) * layout.rows_piece
    width, half = key_w.shape
    stages = out_weight is not None
    shapes = [jax.ShapeDtypeStruct(held[0].shape, jnp.bfloat16)] * 2
    if stages:
        shapes.append(jax.ShapeDtypeStruct((half, out_weight.shape[1]), out_weight.dtype))
    at = 4 + len(pieces) + stages
    return pl.pallas_call(
        functools.partial(project_kernel, layout, first, len(pieces), cases_of(rows_now), stages),
        in_specs=[SCALARS] + [ON_CHIP] * (3 + len(pieces)) + [FAR] * stages + [ON_CHIP] * 2,
        out_specs=[ON_CHIP] * len(shapes),
        out_shape=shapes,
        scratch_shapes=[pltpu.VMEM((rows_now, width), jnp.bfloat16)] * 2 + [pltpu.SemaphoreType.DMA] * stages,
        input_output_aliases={at: 0, at + 1: 1},
        compiler_params=params(28 if stages else 16),
        cost_estimate=cost(4 * rows_now * width * half, 4 * width * half),
        name="project",
    )(plan, gain, key_w, value_w, *pieces, *([out_weight] if stages else []), *held)


def attend_kernel(layout, first, count, cases, plan, gain_ref, key_w_ref, value_w_ref, mask, own_q_ref, other_q_ref,
                  out_w_ref, *refs):
    piece_refs = refs[:count]
    result_refs = refs[count + 2: -4]
    keys_ref, values_ref, raw, rows = refs[-4:]
    append(layout, first, cases_of(raw.shape[0]), plan, piece_refs, gain_ref, key_w_ref, value_w_ref,
           keys_ref, values_ref, raw, rows)
    half, inner = own_q_ref.shape
    heads = inner // DK
    kept = layout.total(plan)

    def attend(number):
        def clear(tile, carry):
            at = pl.ds(pl.multiple_of(tile * TILE, TILE), TILE)
            keys_ref[at, :] = jnp.zeros((TILE, inner), jnp.bfloat16)
            values_ref[at, :] = jnp.zeros((TILE, inner), jnp.bfloat16)
            return carry

        lax.fori_loop(kept, number // TILE, clear, 0)
        ones = jnp.where(
            lax.broadcasted_iota(jnp.int32, (2 * half, DK), 1) == 0, 1.0, 0.0
        ).astype(jnp.bfloat16)

        def scores_of(head):
            here = slice(head * DK, (head + 1) * DK)
            query_rows = jnp.concatenate([own_q_ref[:, here], other_q_ref[:, here]], axis=0)
            return lax.dot_general(
                jnp.concatenate([query_rows, ones], axis=1),
                jnp.concatenate([keys_ref[:number, here], mask[:number, :]], axis=1),
                (((1,), (1,)), ((), ())), preferred_element_type=jnp.float32,
            )

        def weigh(scores):
            expo = jnp.exp(scores - jnp.max(scores, axis=-1, keepdims=True))
            return expo.astype(jnp.bfloat16), jnp.sum(expo, axis=-1, keepdims=True)

        def mix(head, weights, denom):
            mixed = jnp.dot(
                weights, values_ref[:number, head * DK:(head + 1) * DK],
                preferred_element_type=jnp.float32,
            )
            return (mixed * (1.0 / denom)).astype(jnp.bfloat16)

        attended, scores, weighed = [], scores_of(0), None
        for head in range(heads):
            ahead = scores_of(head + 1) if head + 1 < heads else None
            weighing = weigh(scores)
            if weighed is not None:
                attended.append(mix(head - 1, *weighed))
            scores, weighed = ahead, weighing
        attended.append(mix(heads - 1, *weighed))
        product = jnp.dot(
            jnp.concatenate(attended, axis=1), out_w_ref[...], preferred_element_type=jnp.float32
        )
        part = result_refs[0].shape[0]
        for index, result_ref in enumerate(result_refs):
            result_ref[...] = product[index * part:(index + 1) * part, :].astype(jnp.bfloat16)

    low = 0
    for number in cases:
        pl.when((kept * TILE > low) & (kept * TILE <= number))(functools.partial(attend, number))
        low = number


def attend(layout, first, plan, gain, key_w, value_w, mask, own_q, other_q, out_w, pieces, held):
    rows_here, half = own_q.shape
    width = out_w.shape[1]
    enc_rows = layout.tiles * TILE
    cases = [enc_rows * 2 // 3 // 64 * 64, enc_rows]
    result = jax.ShapeDtypeStruct((rows_here // TAIL_PARTS, width), jnp.bfloat16)
    kept = jax.ShapeDtypeStruct(held[0].shape, jnp.bfloat16)
    at = 8 + len(pieces)
    *results, _, _ = pl.pallas_call(
        functools.partial(attend_kernel, layout, first, len(pieces), cases),
        in_specs=[SCALARS] + [ON_CHIP] * (at + 1),
        out_specs=[ON_CHIP] * (2 * TAIL_PARTS + 2),
        out_shape=[result] * (2 * TAIL_PARTS) + [kept, kept],
        scratch_shapes=[pltpu.VMEM((len(pieces) * layout.rows_piece, width), jnp.bfloat16)] * 2,
        input_output_aliases={at: 2 * TAIL_PARTS, at + 1: 2 * TAIL_PARTS + 1},
        compiler_params=params(24),
        cost_estimate=cost(4 * rows_here * (2 * enc_rows + width) * half, 2 * half * width),
        name="attend",
    )(plan, gain, key_w, value_w, mask, own_q, other_q, out_w, *pieces, *held)
    return results[:TAIL_PARTS], results[TAIL_PARTS:]


def on_device(number, queries, passages, enc_gain, key_weight, value_weight, out_weight, passage_length):
    rows_piece = passages.shape[0]
    heads_axis = lax.axis_size("heads")
    chips = number // 2
    cycle = chip_cycle(chips)
    place = {chip: index for index, chip in enumerate(cycle)}
    other_core = [(device, device ^ 1) for device in range(number)]

    def hop(by, crossed=0):
        return [
            (2 * chip + core, 2 * cycle[(place[chip] + by) % chips] + (core ^ crossed))
            for chip in range(chips)
            for core in range(2)
        ]

    def cross(piece):
        return lax.ppermute(piece, "rows", other_core)

    rounds = []
    for distance in range(1, chips // 2 + 1):
        if 2 * distance == chips:
            rounds.append([(-distance, 0), (distance, 1)])
        else:
            rounds.append([(-distance, 0), (distance, 0), (-distance, 1), (distance, 1)])
    order = [(0, 0), (0, 1)] + [source for sources in rounds for source in sources]
    layout = Plan(order, rows_piece, passage_length.shape[0])

    device = lax.axis_index("rows").reshape(1)
    held_rows = number * rows_piece
    crossed = cross(passages)
    ahead = behind = passages
    first, waiting, held, out_w = 2, [], [], None
    for index, sources in enumerate(rounds):
        ahead = lax.ppermute(ahead, "rows", hop(1))
        behind = lax.ppermute(behind, "rows", hop(-1, 1 if len(sources) == 2 else 0))
        if index == 0:
            key_w = stage(device, key_weight, 1)
            ahead, key_w = lax.optimization_barrier((ahead, key_w))
        if index == min(1, len(rounds) - 1):
            plan, gain, value_w, keys, values, own_q, given_q, mask = begin(
                layout, chips, device, passage_length, enc_gain, key_w, value_weight,
                queries, passages, crossed, held_rows,
            )
            held = [keys, values]
        elif index > 1:
            last = index == len(rounds) - 1
            now = len(waiting) if last else 6
            *held, staged = project(
                layout, first, plan, gain, key_w, value_w, waiting[:now], held, out_weight if last else None
            )
            if last:
                out_w = staged
            else:
                held.append(staged)
            first, waiting = first + now, waiting[now:]
        ahead, *held = lax.optimization_barrier((ahead, *held))
        waiting = waiting + ([ahead, behind] if len(sources) == 2 else [ahead, behind, cross(ahead), cross(behind)])
    if out_w is None:
        out_w = stage(device, out_weight, 0)
    other_q = cross(given_q)

    own, other = attend(
        layout, first, plan, gain, key_w, value_w, mask, own_q, other_q, out_w, waiting, held
    )
    received = [cross(part) for part in other]
    shares = [
        (ours.astype(jnp.float32) + theirs.astype(jnp.float32)).astype(jnp.bfloat16)
        for ours, theirs in zip(own, received)
    ]
    by = 1
    while by < heads_axis:
        turn = [(place, place ^ by) for place in range(heads_axis)]
        given = [lax.ppermute(share, "heads", turn) for share in shares]
        shares = [
            (ours.astype(jnp.float32) + theirs.astype(jnp.float32)).astype(jnp.bfloat16)
            for ours, theirs in zip(shares, given)
        ]
        by *= 2
    return jnp.concatenate(shares, axis=0)


def solution(mesh):
    return jax.shard_map(
        functools.partial(on_device, mesh.shape["rows"]),
        mesh=mesh,
        in_specs=(
            P(("groups", "rows"), "heads"),
            P(("groups", "rows"), None),
            P(),
            P(None, "heads"),
            P(None, "heads"),
            P("heads", None),
            P("groups"),
        ),
        out_specs=P(("groups", "rows"), None),
        check_vma=False,
    )
```

```python
import functools

import jax
import jax.numpy as jnp
from jax import lax
from jax.experimental import pallas as pl
from jax.experimental.pallas import tpu as pltpu
from jax.sharding import PartitionSpec as P

DK = 128
PASS_LEN = 256
LOWEST = -1e30
TILE = 16
TAIL_PARTS = 2
WIDE = 1024
ON_CHIP = pl.BlockSpec(memory_space=pltpu.VMEM)
SCALARS = pl.BlockSpec(memory_space=pltpu.SMEM)
FAR = pl.BlockSpec(memory_space=pltpu.HBM)


def params(mib):
    return pltpu.CompilerParams(vmem_limit_bytes=mib * 1024 * 1024)


def cost(flops, moved, exps=0):
    return pl.CostEstimate(flops=flops, bytes_accessed=moved, transcendentals=exps)


def chip_cycle(chips):
    up = list(range(0, chips, 2))
    return up + [chip for chip in range(chips - 1, -1, -1) if chip % 2]


def owner_of(device, source, chips):
    offset, crossed = source
    chip, core = device >> 1, device & 1
    place = jnp.where((chip & 1) == 0, chip >> 1, chips - ((chip + 1) >> 1)) + offset
    place = jnp.where(place < 0, place + chips, jnp.where(place >= chips, place - chips, place))
    chip = jnp.where(place < (chips + 1) >> 1, place << 1, ((chips - place) << 1) - 1)
    return (chip << 1) + (core ^ crossed)


class Plan:
    def __init__(self, order, rows_piece, passages):
        self.order, self.per_piece = order, rows_piece // TILE
        self.rows_piece, self.passages = rows_piece, passages
        self.tiles = len(order) * self.per_piece
        self.size = 2 * self.tiles + 2 + passages

    def write(self, plan, device, length_ref, chips):
        shift = PASS_LEN.bit_length() - 1
        for passage in range(self.passages):
            plan[2 * self.tiles + 2 + passage] = -1
        kept = jnp.int32(0)
        for index, source in enumerate(self.order):
            first = owner_of(device, source, chips) * self.rows_piece
            for tile in range(index * self.per_piece, (index + 1) * self.per_piece):
                row = first + (tile - index * self.per_piece) * TILE
                passage = row >> shift
                here = length_ref[passage] - (row & (PASS_LEN - 1))
                plan[tile] = here
                plan[self.tiles + tile] = kept

                @pl.when((here > 0) & (here < TILE))
                def _(kept=kept, here=here, passage=passage):
                    plan[2 * self.tiles + 2 + passage] = kept * TILE + here

                kept = kept + (here > 0).astype(jnp.int32)
        plan[2 * self.tiles] = kept
        plan[2 * self.tiles + 1] = device & 1

    def here(self, plan, tile):
        return plan[tile]

    def place(self, plan, tile):
        return plan[self.tiles + tile]

    def total(self, plan):
        return plan[2 * self.tiles]

    def core(self, plan):
        return plan[2 * self.tiles + 1]

    def partial(self, plan, passage):
        return plan[2 * self.tiles + 2 + passage]


def keep_valid(layout, plan, first, piece_refs, raw):
    begin = layout.place(plan, first * layout.per_piece)
    after = (first + len(piece_refs)) * layout.per_piece
    for index, piece_ref in enumerate(piece_refs):
        for tile in range(layout.per_piece):
            at = (first + index) * layout.per_piece + tile

            @pl.when(layout.here(plan, at) > 0)
            def _(at=at, tile=tile, piece_ref=piece_ref):
                row = pl.multiple_of((layout.place(plan, at) - begin) * TILE, TILE)
                raw[pl.ds(row, TILE), :] = piece_ref[tile * TILE:(tile + 1) * TILE, :]

    end = layout.place(plan, after) if after < layout.tiles else layout.total(plan)
    return begin, end - begin


def normalize(raw, rows, gain_ref, kept, number):
    wide = raw[:number, :].astype(jnp.float32)
    mean_square = jnp.mean(wide * wide, axis=-1, keepdims=True)
    scaled = wide * lax.rsqrt(mean_square + 1e-06) * gain_ref[...].astype(jnp.float32).reshape(1, -1)
    row = lax.broadcasted_iota(jnp.int32, scaled.shape, 0)
    rows[:number, :] = jnp.where(row < kept * TILE, scaled, 0.0).astype(jnp.bfloat16)


def stage_kernel(axis, device_ref, far, near, sem):
    half = near.shape[axis]
    ours = pl.ds(pl.multiple_of((device_ref[0] & 1) * half, half), half)
    copy = pltpu.make_async_copy(far.at[(slice(None),) * axis + (ours,)], near, sem)
    copy.start()
    copy.wait()


def stage(device, weight, axis):
    shape = tuple(size // 2 if at == axis else size for at, size in enumerate(weight.shape))
    return pl.pallas_call(
        functools.partial(stage_kernel, axis),
        in_specs=[SCALARS, FAR],
        out_specs=ON_CHIP,
        out_shape=jax.ShapeDtypeStruct(shape, weight.dtype),
        scratch_shapes=[pltpu.SemaphoreType.DMA],
        compiler_params=params(48),
        cost_estimate=cost(0, 2 * weight.size),
        name="stage",
    )(device, weight)


def write_mask(layout, plan, mask_ref):
    row = lax.broadcasted_iota(jnp.int32, mask_ref.shape, 0)
    valid = row < layout.total(plan) * TILE
    for passage in range(layout.passages):
        begin = layout.partial(plan, passage)
        end = ((begin + TILE - 1) >> (TILE.bit_length() - 1)) * TILE
        valid = valid & ((begin < 0) | (row < begin) | (row >= end))
    first_column = lax.broadcasted_iota(jnp.int32, mask_ref.shape, 1) == 0
    mask_ref[...] = jnp.where(first_column & ~valid, LOWEST, 0.0).astype(jnp.bfloat16)


def begin_kernel(layout, chips, device_ref, length_far, gain_far, key_w_ref, value_far, queries_far, own_far,
                 crossed_ref, plan, gain_ref, value_w_ref, keys_ref, values_ref, own_q_ref, given_q_ref, mask_ref,
                 length_ref, own_ref, raw, rows, sems):
    device = device_ref[0]
    half = value_w_ref.shape[1]
    ours = pl.ds(pl.multiple_of((device & 1) * half, half), half)
    theirs = pl.ds(pl.multiple_of((1 - (device & 1)) * half, half), half)
    moves = (
        (length_far, length_ref),
        (own_far, own_ref),
        (gain_far, gain_ref),
        (value_far.at[:, ours], value_w_ref),
        (queries_far.at[:, ours], own_q_ref),
        (queries_far.at[:, theirs], given_q_ref),
    )
    copies = [
        pltpu.make_async_copy(source, target, sems.at[index])
        for index, (source, target) in enumerate(moves)
    ]
    for copy in copies:
        copy.start()
    copies[0].wait()
    layout.write(plan, device, length_ref, chips)
    copies[1].wait()
    _, kept = keep_valid(layout, plan, 0, [own_ref, crossed_ref], raw)
    copies[2].wait()
    number = raw.shape[0]
    normalize(raw, rows, gain_ref, kept, number)
    for weight_ref, out_ref in ((key_w_ref, keys_ref), (value_w_ref, values_ref)):
        if weight_ref is value_w_ref:
            write_mask(layout, plan, mask_ref)
            for copy in copies[3:]:
                copy.wait()
        for left in range(0, half, WIDE):
            columns = slice(left, min(left + WIDE, half))
            out_ref[:number, columns] = jnp.dot(
                rows[...], weight_ref[:, columns], preferred_element_type=jnp.float32
            ).astype(jnp.bfloat16)


def begin(layout, chips, device, passage_length, gain, key_w, value_weight, queries, own, crossed, held_rows):
    width, half = key_w.shape
    held = jax.ShapeDtypeStruct((held_rows, half), jnp.bfloat16)
    query_half = jax.ShapeDtypeStruct((queries.shape[0], half), queries.dtype)
    return pl.pallas_call(
        functools.partial(begin_kernel, layout, chips),
        in_specs=[SCALARS, FAR, FAR, ON_CHIP, FAR, FAR, FAR, ON_CHIP],
        out_specs=[SCALARS] + [ON_CHIP] * 7,
        out_shape=[
            jax.ShapeDtypeStruct((layout.size,), jnp.int32),
            jax.ShapeDtypeStruct(gain.shape, gain.dtype),
            jax.ShapeDtypeStruct(key_w.shape, key_w.dtype),
            held, held, query_half, query_half,
            jax.ShapeDtypeStruct((layout.tiles * TILE, DK), jnp.bfloat16),
        ],
        scratch_shapes=[
            pltpu.SMEM(passage_length.shape, jnp.int32),
            pltpu.VMEM(own.shape, own.dtype),
            pltpu.VMEM((2 * own.shape[0], width), jnp.bfloat16),
            pltpu.VMEM((2 * own.shape[0], width), jnp.bfloat16),
            pltpu.SemaphoreType.DMA((6,)),
        ],
        compiler_params=params(36),
        cost_estimate=cost(8 * own.shape[0] * width * half, 8 * width * half),
        name="begin",
    )(device, passage_length, gain, key_w, value_weight, queries, own, crossed)


def append(layout, first, cases, plan, piece_refs, gain_ref, key_w_ref, value_w_ref, keys_ref, values_ref, raw, rows):
    begin_tile, kept = keep_valid(layout, plan, first, piece_refs, raw)
    start = pl.multiple_of(begin_tile * TILE, TILE)
    width = key_w_ref.shape[1]

    def project(number):
        normalize(raw, rows, gain_ref, kept, number)
        for left in range(0, width, WIDE):
            columns = slice(left, min(left + WIDE, width))
            for weight_ref, out_ref in ((key_w_ref, keys_ref), (value_w_ref, values_ref)):
                out_ref[pl.ds(start, number), columns] = jnp.dot(
                    rows[:number, :], weight_ref[:, columns], preferred_element_type=jnp.float32
                ).astype(jnp.bfloat16)

    low = 0
    for number in cases:
        pl.when((kept * TILE > low) & (kept * TILE <= number))(functools.partial(project, number))
        low = number


def cases_of(rows_now):
    return list(range(rows_now, rows_now // 3, -64))[::-1]


def project_kernel(layout, first, count, cases, stages, plan, gain_ref, key_w_ref, value_w_ref, *refs):
    piece_refs = refs[:count]
    if stages:
        out_far, out_w_ref, sem = refs[count], refs[-4], refs[-1]
        refs = refs[:-4] + refs[-3:-1]
        half = out_w_ref.shape[0]
        ours = pl.ds(pl.multiple_of(layout.core(plan) * half, half), half)
        staging = pltpu.make_async_copy(out_far.at[ours, :], out_w_ref, sem)
        staging.start()
    keys_ref, values_ref, raw, rows = refs[-4:]
    append(layout, first, cases, plan, piece_refs, gain_ref, key_w_ref, value_w_ref, keys_ref, values_ref, raw, rows)
    if stages:
        staging.wait()


def project(layout, first, plan, gain, key_w, value_w, pieces, held, out_weight=None):
    rows_now = len(pieces) * layout.rows_piece
    width, half = key_w.shape
    stages = out_weight is not None
    shapes = [jax.ShapeDtypeStruct(held[0].shape, jnp.bfloat16)] * 2
    if stages:
        shapes.append(jax.ShapeDtypeStruct((half, out_weight.shape[1]), out_weight.dtype))
    at = 4 + len(pieces) + stages
    return pl.pallas_call(
        functools.partial(project_kernel, layout, first, len(pieces), cases_of(rows_now), stages),
        in_specs=[SCALARS] + [ON_CHIP] * (3 + len(pieces)) + [FAR] * stages + [ON_CHIP] * 2,
        out_specs=[ON_CHIP] * len(shapes),
        out_shape=shapes,
        scratch_shapes=[pltpu.VMEM((rows_now, width), jnp.bfloat16)] * 2 + [pltpu.SemaphoreType.DMA] * stages,
        input_output_aliases={at: 0, at + 1: 1},
        compiler_params=params(28 if stages else 16),
        cost_estimate=cost(4 * rows_now * width * half, 4 * width * half),
        name="project",
    )(plan, gain, key_w, value_w, *pieces, *([out_weight] if stages else []), *held)


def attend_kernel(layout, first, count, cases, plan, gain_ref, key_w_ref, value_w_ref, mask, own_q_ref, other_q_ref,
                  out_w_ref, *refs):
    piece_refs = refs[:count]
    result_refs = refs[count + 2: -4]
    keys_ref, values_ref, raw, rows = refs[-4:]
    append(layout, first, cases_of(raw.shape[0]), plan, piece_refs, gain_ref, key_w_ref, value_w_ref,
           keys_ref, values_ref, raw, rows)
    half, inner = own_q_ref.shape
    heads = inner // DK
    kept = layout.total(plan)

    def attend(number):
        def clear(tile, carry):
            at = pl.ds(pl.multiple_of(tile * TILE, TILE), TILE)
            keys_ref[at, :] = jnp.zeros((TILE, inner), jnp.bfloat16)
            values_ref[at, :] = jnp.zeros((TILE, inner), jnp.bfloat16)
            return carry

        lax.fori_loop(kept, number // TILE, clear, 0)
        ones = jnp.where(
            lax.broadcasted_iota(jnp.int32, (2 * half, DK), 1) == 0, 1.0, 0.0
        ).astype(jnp.bfloat16)

        def scores_of(head):
            here = slice(head * DK, (head + 1) * DK)
            query_rows = jnp.concatenate([own_q_ref[:, here], other_q_ref[:, here]], axis=0)
            return lax.dot_general(
                jnp.concatenate([query_rows, ones], axis=1),
                jnp.concatenate([keys_ref[:number, here], mask[:number, :]], axis=1),
                (((1,), (1,)), ((), ())), preferred_element_type=jnp.float32,
            )

        def weigh(scores):
            expo = jnp.exp(scores - jnp.max(scores, axis=-1, keepdims=True))
            return expo.astype(jnp.bfloat16), jnp.sum(expo, axis=-1, keepdims=True)

        def mix(head, weights, denom):
            mixed = jnp.dot(
                weights, values_ref[:number, head * DK:(head + 1) * DK],
                preferred_element_type=jnp.float32,
            )
            return (mixed * (1.0 / denom)).astype(jnp.bfloat16)

        attended, scores, weighed = [], scores_of(0), None
        for head in range(heads):
            ahead = scores_of(head + 1) if head + 1 < heads else None
            weighing = weigh(scores)
            if weighed is not None:
                attended.append(mix(head - 1, *weighed))
            scores, weighed = ahead, weighing
        attended.append(mix(heads - 1, *weighed))
        product = jnp.dot(
            jnp.concatenate(attended, axis=1), out_w_ref[...], preferred_element_type=jnp.float32
        )
        part = result_refs[0].shape[0]
        for index, result_ref in enumerate(result_refs):
            result_ref[...] = product[index * part:(index + 1) * part, :].astype(jnp.bfloat16)

    low = 0
    for number in cases:
        pl.when((kept * TILE > low) & (kept * TILE <= number))(functools.partial(attend, number))
        low = number


def attend(layout, first, plan, gain, key_w, value_w, mask, own_q, other_q, out_w, pieces, held, lone):
    rows_here, half = own_q.shape
    width = out_w.shape[1]
    enc_rows = layout.tiles * TILE
    most = enc_rows - (PASS_LEN - PASS_LEN // 4 if lone else 0)
    cases = [enc_rows * 2 // 3 // 64 * 64, most]
    result = jax.ShapeDtypeStruct((rows_here // TAIL_PARTS, width), jnp.bfloat16)
    kept = jax.ShapeDtypeStruct(held[0].shape, jnp.bfloat16)
    at = 8 + len(pieces)
    *results, _, _ = pl.pallas_call(
        functools.partial(attend_kernel, layout, first, len(pieces), cases),
        in_specs=[SCALARS] + [ON_CHIP] * (at + 1),
        out_specs=[ON_CHIP] * (2 * TAIL_PARTS + 2),
        out_shape=[result] * (2 * TAIL_PARTS) + [kept, kept],
        scratch_shapes=[pltpu.VMEM((len(pieces) * layout.rows_piece, width), jnp.bfloat16)] * 2,
        input_output_aliases={at: 2 * TAIL_PARTS, at + 1: 2 * TAIL_PARTS + 1},
        compiler_params=params(24),
        cost_estimate=cost(4 * rows_here * (2 * enc_rows + width) * half, 2 * half * width),
        name="attend",
    )(plan, gain, key_w, value_w, mask, own_q, other_q, out_w, *pieces, *held)
    return results[:TAIL_PARTS], results[TAIL_PARTS:]


def on_device(number, queries, passages, enc_gain, key_weight, value_weight, out_weight, passage_length):
    rows_piece = passages.shape[0]
    heads_axis = lax.axis_size("heads")
    chips = number // 2
    cycle = chip_cycle(chips)
    place = {chip: index for index, chip in enumerate(cycle)}
    other_core = [(device, device ^ 1) for device in range(number)]

    def hop(by, crossed=0):
        return [
            (2 * chip + core, 2 * cycle[(place[chip] + by) % chips] + (core ^ crossed))
            for chip in range(chips)
            for core in range(2)
        ]

    def cross(piece):
        return lax.ppermute(piece, "rows", other_core)

    rounds = []
    for distance in range(1, chips // 2 + 1):
        if 2 * distance == chips:
            rounds.append([(-distance, 0), (distance, 1)])
        else:
            rounds.append([(-distance, 0), (distance, 0), (-distance, 1), (distance, 1)])
    order = [(0, 0), (0, 1)] + [source for sources in rounds for source in sources]
    layout = Plan(order, rows_piece, passage_length.shape[0])

    device = lax.axis_index("rows").reshape(1)
    held_rows = number * rows_piece
    crossed = cross(passages)
    ahead = behind = passages
    first, waiting, held, out_w = 2, [], [], None
    for index, sources in enumerate(rounds):
        ahead = lax.ppermute(ahead, "rows", hop(1))
        behind = lax.ppermute(behind, "rows", hop(-1, 1 if len(sources) == 2 else 0))
        if index == 0:
            key_w = stage(device, key_weight, 1)
            ahead, key_w = lax.optimization_barrier((ahead, key_w))
        if index == min(1, len(rounds) - 1):
            plan, gain, value_w, keys, values, own_q, given_q, mask = begin(
                layout, chips, device, passage_length, enc_gain, key_w, value_weight,
                queries, passages, crossed, held_rows,
            )
            held = [keys, values]
        elif index > 1:
            last = index == len(rounds) - 1
            now = len(waiting) if last else 6
            *held, staged = project(
                layout, first, plan, gain, key_w, value_w, waiting[:now], held, out_weight if last else None
            )
            if last:
                out_w = staged
            else:
                held.append(staged)
            first, waiting = first + now, waiting[now:]
        ahead, *held = lax.optimization_barrier((ahead, *held))
        waiting = waiting + ([ahead, behind] if len(sources) == 2 else [ahead, behind, cross(ahead), cross(behind)])
    if out_w is None:
        out_w = stage(device, out_weight, 0)
    other_q = cross(given_q)

    own, other = attend(
        layout, first, plan, gain, key_w, value_w, mask, own_q, other_q, out_w, waiting, held,
        lax.axis_size("groups") == 1,
    )
    received = [cross(part) for part in other]
    shares = [
        (ours.astype(jnp.float32) + theirs.astype(jnp.float32)).astype(jnp.bfloat16)
        for ours, theirs in zip(own, received)
    ]
    by = 1
    while by < heads_axis:
        turn = [(place, place ^ by) for place in range(heads_axis)]
        given = [lax.ppermute(share, "heads", turn) for share in shares]
        shares = [
            (ours.astype(jnp.float32) + theirs.astype(jnp.float32)).astype(jnp.bfloat16)
            for ours, theirs in zip(shares, given)
        ]
        by *= 2
    return jnp.concatenate(shares, axis=0)


def solution(mesh):
    return jax.shard_map(
        functools.partial(on_device, mesh.shape["rows"]),
        mesh=mesh,
        in_specs=(
            P(("groups", "rows"), "heads"),
            P(("groups", "rows"), None),
            P(),
            P(None, "heads"),
            P(None, "heads"),
            P("heads", None),
            P("groups"),
        ),
        out_specs=P(("groups", "rows"), None),
        check_vma=False,
    )
```
